256 devices in a mesh: dp: 4 (over y), expert: 64 (over x, z, core).
Axes of the slice: x: 4, y: 4, z: 8, core: 2. Of those that a mesh axis runs over, the one named last changes fastest.
Arguments:
- tokens: bfloat16 [32768, 2048], P(('dp', 'expert')), may hold values from -24 to 24
- routes: int32 [32768, 8], P(('dp', 'expert')), may hold values from 0 to 63, all different within a row; in each aligned block of 128 rows (0 to 127, 128 to 255, ...) at most 20 rows name the same one
- gate_values: float32 [32768, 8], P(('dp', 'expert')), may hold values from 0.05 to 1
- latent_down: bfloat16 [2048, 512], replicated, may hold values from -0.125 to 0.125
- gate_weight: bfloat16 [64, 512, 1024], P('expert'), may hold values from -0.25 to 0.25
- up_weight: bfloat16 [64, 512, 1024], P('expert'), may hold values from -0.25 to 0.25
- out_weight: bfloat16 [64, 1024, 512], P('expert'), may hold values from -0.1875 to 0.1875
- latent_up: bfloat16 [2048, 512], replicated, may hold values from -0.25 to 0.25
- grad_mixed: bfloat16 [32768, 2048], P(('dp', 'expert')), may hold values from -24 to 24
Outputs:
- mixed: bfloat16 [32768, 2048], P(('dp', 'expert'))
- grad_tokens: bfloat16 [32768, 2048], P(('dp', 'expert'))
- grad_latent_down: float32 [2048, 512], P('expert')
- grad_latent_up: float32 [2048, 512], P('expert')
- grad_gate_weight: float32 [64, 512, 1024], P('expert', None, 'dp')
- grad_up_weight: float32 [64, 512, 1024], P('expert', None, 'dp')
- grad_out_weight: float32 [64, 1024, 512], P('expert', 'dp')
The draws below stay inside these ranges and needn't reach their ends.
Inputs may be any that keep to these rules, and one draw needn't show every extreme that they name: `routes`: each row names 8 different experts. Within the 128 rows of one device no expert is named by more than 20 rows, a bound that some block reaches.
All inputs are finite; a program needn't handle non-finite values.
Results may differ from the reference program's by a relative error of at most 0.02.
Values may be sent and summed in bfloat16 or wider, within the bound.
A program may use at most 128 MiB of HBM per device.

```python
import math
import jax
import jax.numpy as jnp
import numpy as np
from jax import lax

D = 2048
LATENT = 512
HIDDEN_SIZE = 1024
TOPK = 8
TOK_DEV = 128
EXPERTS = 64
CAP = 20
TOKENS = 32768


def with_spikes(array, rng, source, target, parts, factor):
    def block_of(axis_at):
        return (jnp.arange(array.shape[axis_at]) // (array.shape[axis_at] // parts)).reshape((-1,) + (1,) * (array.ndim - 1 - axis_at))

    first = jax.random.permutation(rng, parts)[block_of(target)]
    second = (block_of(target) + parts // 2) % parts
    return jnp.where((block_of(source) == first) | (block_of(source) == second), factor * array, array)


def shard_levels(stream_key, extent, cuts, smallest, high):
    factor_of, own = 1.0, jax.random.fold_in(stream_key, 6)
    for axis_at, blocks in cuts:
        heights = jnp.exp(jax.random.uniform(jax.random.fold_in(own, axis_at), (blocks,), jnp.float32, smallest / len(cuts), high / len(cuts)))
        factor_of = factor_of * jnp.repeat(heights, extent[axis_at] // blocks).reshape([-1 if axis == axis_at else 1 for axis in range(len(extent))])
    return factor_of


def deal_out(rng, own, number, rows, number_of, top, limit, slope):
    sequence = jax.random.permutation(rng, number_of)
    packed, common = load_shares(number_of, rows * top, limit, slope, True), load_shares(number_of, rows * top, limit, slope, False)
    places = jnp.arange(number_of)

    def named(tallies, turn):
        used = int((tallies > 0).sum())
        fixed = max(1, used // 4)
        shifted = fixed + (places - fixed + turn * (used - fixed)) % max(1, number_of - fixed)
        return jnp.zeros((number_of,), jnp.int32).at[sequence[jnp.where(places < fixed, places, shifted)]].set(jnp.asarray(tallies, jnp.int32))

    tallies = jnp.where(number % 4 == 0, named(packed, number // 4), named(common, number - number // 4 - 1))
    mixed = jax.random.permutation(jax.random.fold_in(own, 3), number_of)
    source_of, sink = mixed[0:number_of // 2 * 2:2], mixed[1:number_of // 2 * 2:2]
    room = jnp.minimum(tallies[source_of] - 1, limit - tallies[sink]) // 2
    room = jnp.where((source_of == sequence[0]) | (sink == sequence[0]) | (tallies[sink] == 0), 0, jnp.maximum(room, 0))
    shifted = jax.random.randint(jax.random.fold_in(own, 4), (number_of // 2,), 0, 1 << 20) % (room + 1)
    tallies = tallies.at[source_of].add(-shifted).at[sink].add(shifted)
    labels = jnp.searchsorted(jnp.cumsum(tallies), jnp.arange(rows * top), side="right").astype(jnp.int32)
    table = labels.reshape(top, rows).T
    table = table[jax.random.permutation(jax.random.fold_in(own, 1), rows)]
    turn = jax.random.randint(jax.random.fold_in(own, 2), (rows, 1), 0, top)
    return jnp.take_along_axis(table, (jnp.arange(top)[None, :] + turn) % top, axis=1)


def load_shares(count, total, limit, skew, full):
    loads = [(1 << 20) // math.isqrt(rank ** skew) + 1 for rank in range(1, count + 1)]
    largest = limit if full else min(limit, max(-(-total // count), total * loads[0] // sum(loads)))
    least = 1 if total - largest >= count - 1 else 0
    given, spare = [largest] + [least] * (count - 1), total - largest - least * (count - 1)
    while spare > 0:
        free = [i for i in range(1, count) if given[i] < largest] or [i for i in range(1, count) if given[i] < limit]
        mass, left = sum([loads[i] for i in free]), spare
        for i in free:
            addition = min(limit - given[i], max(1, left * loads[i] // mass), spare)
            given[i] = given[i] + addition
            spare = spare - addition
    return np.array(given)


def gaussian(stream_key, shape, width, limit, cuts=(), held_as=jnp.bfloat16):
    values = jax.random.normal(stream_key, shape, jnp.float32) * width
    if len(cuts) > 0:
        values = shard_levels(stream_key, shape, cuts, -0.22, 0.18) * values
    return jnp.clip(values, min=-limit, max=limit).astype(held_as)


def gaussian_with(rng, shape, spread, most, shards, heavy, kind=jnp.bfloat16):
    array = spread * jax.random.normal(rng, shape, jnp.float32)
    if shards:
        array = array * shard_levels(rng, shape, shards, -0.22, 0.18)
    return jnp.clip(with_spikes(array, jax.random.fold_in(rng, 3), *heavy), -most, most).astype(kind)


def setup_inputs(seed: int = 0) -> dict:
    seeds = jax.random.split(jax.random.key(seed), 10)
    tokens = gaussian_with(seeds[0], (TOKENS, D), 1.0, 24.0, ((0, 256),), (0, 1, 256, 6.0))
    routes_keys = jax.random.split(jax.random.fold_in(seeds[1], 1), TOKENS // TOK_DEV)
    routes_turns = jax.random.permutation(jax.random.fold_in(seeds[1], 3), TOKENS // TOK_DEV)
    routes = jax.vmap(lambda own, number: deal_out(jax.random.fold_in(seeds[1], 2), own, number, TOK_DEV, EXPERTS, TOPK, CAP, 2))(routes_keys, routes_turns).reshape((TOKENS, TOPK))
    gate_values = jnp.clip(jnp.exp(math.log(1.0) - 2.9957323 * jax.random.uniform(seeds[2], (TOKENS, TOPK), jnp.float32) ** shard_levels(seeds[2], (TOKENS, TOPK), ((0, 256),), -0.2, 0.2)), 0.05, 1.0)
    latent_down = gaussian(seeds[3], (D, LATENT), D ** -0.5, 0.125)
    gate_weight = gaussian(seeds[4], (EXPERTS, LATENT, HIDDEN_SIZE), LATENT ** -0.5, 0.25, ((0, 64),))
    up_weight = gaussian(seeds[5], (EXPERTS, LATENT, HIDDEN_SIZE), LATENT ** -0.5, 0.25, ((0, 64),))
    out_weight = gaussian(seeds[6], (EXPERTS, HIDDEN_SIZE, LATENT), HIDDEN_SIZE ** -0.5, 0.1875, ((0, 64),))
    latent_up = gaussian(seeds[7], (D, LATENT), LATENT ** -0.5, 0.25)
    grad_mixed = gaussian_with(seeds[8], (TOKENS, D), 1.0, 24.0, ((0, 256),), (0, 1, 256, 6.0))
    return {"tokens": tokens, "routes": routes, "gate_values": gate_values, "latent_down": latent_down, "gate_weight": gate_weight, "up_weight": up_weight, "out_weight": out_weight, "latent_up": latent_up, "grad_mixed": grad_mixed}


CONTRACT_ROWS = (((0,), (0,)), ((), ()))
CONTRACT_COLS = (((1,), (1,)), ((), ()))


def expert_math(rows_in, grad_rows, gate_matrix, up_matrix, out_matrix):
    pre_gate = jnp.dot(rows_in, gate_matrix, preferred_element_type=jnp.float32)
    pre_up = jnp.dot(rows_in, up_matrix, preferred_element_type=jnp.float32)
    sigmoid_gate = jax.nn.sigmoid(pre_gate)
    swish_gate = pre_gate * sigmoid_gate
    activation = (swish_gate * pre_up).astype(jnp.bfloat16)
    expert_out = jnp.dot(activation, out_matrix, preferred_element_type=jnp.float32).astype(jnp.bfloat16)
    grad_act = lax.dot_general(grad_rows, out_matrix, CONTRACT_COLS, preferred_element_type=jnp.float32)
    grad_gate = (grad_act * pre_up * sigmoid_gate * (1.0 + pre_gate * (1.0 - sigmoid_gate))).astype(jnp.bfloat16)
    grad_up = (grad_act * swish_gate).astype(jnp.bfloat16)
    grad_back = lax.dot_general(grad_gate, gate_matrix, CONTRACT_COLS, preferred_element_type=jnp.float32)
    grad_back = grad_back + lax.dot_general(grad_up, up_matrix, CONTRACT_COLS, preferred_element_type=jnp.float32)
    return expert_out, grad_back.astype(jnp.bfloat16), activation, grad_gate, grad_up


def reference(tokens, routes, gate_values, latent_down, gate_weight, up_weight, out_weight, latent_up, grad_mixed):
    latent = jnp.dot(tokens, latent_down, preferred_element_type=jnp.float32).astype(jnp.bfloat16)
    grad_comb = jnp.dot(grad_mixed, latent_up, preferred_element_type=jnp.float32)
    blocks = TOKENS // TOK_DEV
    per_block = routes.reshape(blocks, TOK_DEV * TOPK)
    onehot = (per_block[:, :, None] == jnp.arange(EXPERTS, dtype=jnp.int32)[None, None, :]).astype(jnp.int32)
    before = jnp.cumsum(onehot, axis=1, dtype=jnp.int32) - onehot
    slot_index = jnp.sum(before * onehot, axis=2, dtype=jnp.int32)
    place = jnp.arange(blocks, dtype=jnp.int32)[:, None] * CAP + slot_index
    row_ids = jnp.arange(TOKENS * TOPK, dtype=jnp.int32).reshape(blocks, TOK_DEV * TOPK)
    table = jnp.zeros((EXPERTS, blocks * CAP), jnp.int32).at[per_block, place].set(row_ids + 1)
    flat_gates = gate_values.reshape(-1)

    def one_expert(totals, pieces):
        comb_total, grad_total = totals
        table_rows, gate_matrix, up_matrix, out_matrix = pieces
        filled = table_rows > 0
        source_row = jnp.maximum(table_rows - 1, 0).astype(jnp.int32)
        token_row = (source_row // TOPK).astype(jnp.int32)
        rows_in = jnp.where(filled[:, None], latent[token_row], jnp.zeros((), latent.dtype))
        scaled = (flat_gates[source_row][:, None] * grad_comb[token_row]).astype(jnp.bfloat16)
        grad_rows = jnp.where(filled[:, None], scaled, jnp.zeros((), scaled.dtype))
        expert_out, grad_back, activation, grad_gate, grad_up = expert_math(rows_in, grad_rows, gate_matrix, up_matrix, out_matrix)
        weight = jnp.where(filled, flat_gates[source_row], jnp.zeros((), flat_gates.dtype))
        comb_total = comb_total.at[token_row].add(weight[:, None] * expert_out.astype(jnp.float32))
        grad_total = grad_total.at[token_row].add(jnp.where(filled[:, None], grad_back.astype(jnp.float32), jnp.zeros((), jnp.float32)))
        gate_grad = lax.dot_general(rows_in, grad_gate, CONTRACT_ROWS, preferred_element_type=jnp.float32)
        up_grad = lax.dot_general(rows_in, grad_up, CONTRACT_ROWS, preferred_element_type=jnp.float32)
        out_grad = lax.dot_general(activation, grad_rows, CONTRACT_ROWS, preferred_element_type=jnp.float32)
        return (comb_total, grad_total), (gate_grad, up_grad, out_grad)

    initial = (jnp.zeros((TOKENS, LATENT), jnp.float32), jnp.zeros((TOKENS, LATENT), jnp.float32))
    totals, grads = lax.scan(one_expert, initial, (table, gate_weight, up_weight, out_weight))
    combined = totals[0].astype(jnp.bfloat16)
    grad_latent = totals[1].astype(jnp.bfloat16)
    mixed = lax.dot_general(combined, latent_up, CONTRACT_COLS, preferred_element_type=jnp.float32).astype(jnp.bfloat16)
    grad_tokens = lax.dot_general(grad_latent, latent_down, CONTRACT_COLS, preferred_element_type=jnp.float32).astype(jnp.bfloat16)
    grad_latent_down = lax.dot_general(tokens, grad_latent, CONTRACT_ROWS, preferred_element_type=jnp.float32)
    grad_latent_up = lax.dot_general(grad_mixed, combined, CONTRACT_ROWS, preferred_element_type=jnp.float32)
    return (mixed, grad_tokens, grad_latent_down, grad_latent_up, grads[0], grads[1], grads[2])
```

```python
from functools import partial

import jax
import jax.numpy as jnp
from jax import lax
from jax.experimental import pallas as pl
from jax.experimental.pallas import tpu as pltpu
from jax.sharding import PartitionSpec as P

MESH = pl.DeviceIdType.MESH
ROWS = (((0,), (0,)), ((), ()))
COLS = (((1,), (1,)), ((), ()))
PLAIN = (((1,), (0,)), ((), ()))
F32 = jnp.float32
BF16 = jnp.bfloat16

RING = 8
CORES = 2
CAP = 20
MAIN = 16
EXTRA = 4
SET = 4
SET_ROWS = SET * CAP


def dot(a, b, dims=PLAIN):
    return lax.dot_general(a, b, dims, preferred_element_type=F32)


def layer_kernel(
    ring,
    routes_ref,
    gates_ref,
    tokens_ref,
    cotan_ref,
    down_ref,
    up_ref,
    gw_ref,
    uw_ref,
    ow_ref,
    mid_ref,
    gate_grad_ref,
    up_grad_ref,
    out_grad_ref,
    gathered,
    send_rows,
    expert_rows,
    result_rows,
    back_rows,
    pick,
    weigh,
    extra_sum,
    act,
    grad_gate,
    grad_up,
    ring_out,
    ring_in,
    grads_out,
    grads_in,
    gather_send,
    gather_recv,
    slot_send,
    slot_recv,
    back_send,
    back_recv,
    own_sem,
    ring_send,
    ring_recv,
    grad_send,
    grad_recv,
):
    tokens_here, latent = tokens_ref.shape[0], down_ref.shape[1]
    hidden = gw_ref.shape[1]
    experts = lax.axis_size("expert")
    groups = lax.axis_size("dp")
    columns = experts // (ring * CORES)
    peers = columns * CORES
    half = ring // 2
    sets = ring // SET
    me = lax.axis_index("expert")
    my_group = lax.axis_index("dp")
    z = lax.rem(lax.div(me, CORES), ring)
    core = lax.rem(me, CORES)
    place = lax.div(me, ring * CORES) * CORES + core

    def on_ring(step):
        other = lax.rem(z + step + ring, ring)
        return (my_group, me + (other - z) * CORES)

    def at_peer(d):
        return (my_group, (lax.div(d, CORES) * ring + z) * CORES + lax.rem(d, CORES))

    def peer(j):
        return lax.rem(place + j, peers)

    def group_at(k):
        return (lax.rem(my_group + k, groups), me)

    barrier = pltpu.get_barrier_semaphore()
    for step in (1, -1):
        pl.semaphore_signal(barrier, inc=1, device_id=on_ring(step), device_id_type=MESH)
    for j in range(1, peers):
        pl.semaphore_signal(barrier, inc=1, device_id=at_peer(peer(j)), device_id_type=MESH)
    for k in range(1, groups):
        pl.semaphore_signal(barrier, inc=1, device_id=group_at(k), device_id_type=MESH)

    gathered[0, 0:tokens_here, 0:latent] = dot(tokens_ref[...], down_ref[...]).astype(BF16)
    gathered[0, 0:tokens_here, latent:] = dot(cotan_ref[...], up_ref[...]).astype(BF16)
    expert_ids = lax.broadcasted_iota(jnp.int32, (experts, tokens_here), 0)
    table = jnp.zeros((experts, tokens_here), F32)
    for k in range(routes_ref.shape[0]):
        table = table + jnp.where(expert_ids == routes_ref[k : k + 1, :], gates_ref[k : k + 1, :], 0.0)
    table_high = table.astype(BF16)
    table_low = (table - table_high.astype(F32)).astype(BF16)
    per_column = ring * CORES
    for b in range(columns):
        rows = slice(b * per_column, (b + 1) * per_column)
        lanes = slice(b * tokens_here, (b + 1) * tokens_here)
        low_lanes = slice(latent + b * tokens_here, latent + (b + 1) * tokens_here)
        gathered[0, tokens_here : tokens_here + per_column, lanes] = table_high[rows, :]
        gathered[0, tokens_here : tokens_here + per_column, low_lanes] = table_low[rows, :]

    pl.semaphore_wait(barrier, 2 + (peers - 1) + (groups - 1))

    def gather_copy(way, step):
        target = on_ring(1 if way == 0 else -1)
        source = 0 if step == 0 else 2 * step - 1 + way
        if step < half - 1:
            src, dst = gathered.at[source], gathered.at[2 * step + 1 + way]
        else:
            lanes = pl.ds(way * latent, latent)
            src, dst = gathered.at[source, :, lanes], gathered.at[ring - 1, :, lanes]
        return pltpu.make_async_remote_copy(
            src_ref=src,
            dst_ref=dst,
            send_sem=gather_send.at[way, step],
            recv_sem=gather_recv.at[way, step],
            device_id=target,
            device_id_type=MESH,
        )

    earlier = (
        lax.broadcasted_iota(jnp.int32, (tokens_here, tokens_here), 0)
        < lax.broadcasted_iota(jnp.int32, (tokens_here, tokens_here), 1)
    ).astype(BF16)
    row_ids = lax.broadcasted_iota(jnp.int32, (per_column, tokens_here), 0)
    main_slots = lax.broadcasted_iota(jnp.int32, (MAIN, tokens_here), 0).astype(F32)

    def slot_copy(j, s, first, count):
        d = peer(j)
        rows = pl.ds(s * SET_ROWS + first, count)
        return pltpu.make_async_remote_copy(
            src_ref=send_rows.at[d, rows],
            dst_ref=expert_rows.at[place, rows],
            send_sem=slot_send.at[s, j],
            recv_sem=slot_recv.at[s, j],
            device_id=at_peer(d),
            device_id_type=MESH,
        )

    def own_slots(s, first, count):
        rows = pl.ds(s * SET_ROWS + first, count)
        return pltpu.make_async_copy(
            send_rows.at[place, rows], expert_rows.at[place, rows], own_sem.at[0, s]
        )

    def dispatch(i):
        s, within = i // SET, i % SET
        weights = []
        for b in range(columns):
            info = (
                gathered[i, tokens_here : tokens_here + per_column, b * tokens_here : (b + 1) * tokens_here].astype(F32)
                + gathered[
                    i,
                    tokens_here : tokens_here + per_column,
                    latent + b * tokens_here : latent + (b + 1) * tokens_here,
                ].astype(F32)
            )
            for c in range(CORES):
                weights.append(
                    jnp.sum(jnp.where(row_ids == z * CORES + c, info, 0.0), axis=0, keepdims=True)
                )
        weight = jnp.concatenate(weights, axis=0)
        named = weight > 0.0
        before = dot(named.astype(F32).astype(BF16), earlier)
        slot = jnp.where(named, before, -1.0)
        extra_rows = lax.broadcasted_iota(jnp.int32, (MAIN, tokens_here), 0)
        extra_slots = jnp.where(
            lax.div(extra_rows, EXTRA) == within, MAIN + lax.rem(extra_rows, EXTRA), -2
        ).astype(F32)
        hits = []
        for slots in (main_slots, extra_slots):
            for d in range(peers):
                hits.append((slots == slot[d : d + 1, :]).astype(F32))
        chosen = jnp.concatenate(hits, axis=0)
        weight_rows = jnp.concatenate(
            [jnp.broadcast_to(weight[d : d + 1, :], (MAIN, tokens_here)) for d in range(peers)], axis=0
        )
        weighted = chosen * jnp.concatenate([weight_rows, weight_rows], axis=0)
        pick[i] = chosen.astype(BF16)
        weigh[i] = weighted.astype(BF16)
        scale = jnp.sum(weighted, axis=1, keepdims=True)
        chosen = chosen.astype(BF16)
        main_count = peers * MAIN
        for part in range(2):
            lanes = slice(part * latent, (part + 1) * latent)
            rows = dot(chosen, gathered[i, 0:tokens_here, lanes])
            if part == 1:
                rows = rows * scale
            first = s * SET_ROWS + within * MAIN
            send_rows[:, first : first + MAIN, lanes] = (
                rows[:main_count].astype(BF16).reshape(peers, MAIN, latent)
            )
            extra = rows[main_count:]
            if within > 0:
                extra = extra + extra_sum[:, lanes]
            if within < SET - 1:
                extra_sum[:, lanes] = extra
            else:
                first = s * SET_ROWS + SET * MAIN
                send_rows[:, first : first + MAIN, lanes] = extra.astype(BF16).reshape(peers, MAIN, latent)
        count = MAIN if within < SET - 1 else 2 * MAIN

        def start(j, carry):
            slot_copy(j, s, within * MAIN, count).start()
            return carry

        lax.fori_loop(1, peers, start, 0)
        own_slots(s, within * MAIN, count).start()

    for way in range(2):
        gather_copy(way, 0).start()
    dispatch(0)
    for step in range(1, half):
        for way in range(2):
            gather_copy(way, step - 1).wait_recv()
            gather_copy(way, step).start()
        for way in range(2):
            dispatch(2 * step - 1 + way)
    for way in range(2):
        gather_copy(way, half - 1).wait_recv()
    dispatch(ring - 1)

    def back_copy(j, s):
        d = peer(j)
        rows = pl.ds(s * SET_ROWS, SET_ROWS)
        return pltpu.make_async_remote_copy(
            src_ref=result_rows.at[d, rows],
            dst_ref=back_rows.at[place, rows],
            send_sem=back_send.at[s, j],
            recv_sem=back_recv.at[s, j],
            device_id=at_peer(d),
            device_id_type=MESH,
        )

    def own_back(s):
        rows = pl.ds(s * SET_ROWS, SET_ROWS)
        return pltpu.make_async_copy(result_rows.at[place, rows], back_rows.at[place, rows], own_sem.at[1, s])

    tile = min(256, hidden)
    wide = min(256, latent)
    count = peers * SET_ROWS

    def expert(s):
        def arrived(j, carry):
            slot_copy(j, s, 0, SET_ROWS).wait_recv()
            return carry

        lax.fori_loop(1, peers, arrived, 0)
        own_slots(s, 0, SET_ROWS).wait()
        set_rows = slice(s * SET_ROWS, (s + 1) * SET_ROWS)

        def hidden_tile(h, carry):
            cols = pl.ds(pl.multiple_of(h * tile, tile), tile)
            rows_in = expert_rows[:, set_rows, 0:latent].reshape(count, latent)
            grad_in = expert_rows[:, set_rows, latent:].reshape(count, latent)
            pre_gate = dot(rows_in, gw_ref[:, cols])
            pre_up = dot(rows_in, uw_ref[:, cols])
            grad_act = dot(grad_in, ow_ref[cols, :], COLS)
            sig = 1.0 / (1.0 + jnp.exp(-pre_gate))
            swish = pre_gate * sig
            shape = (peers, SET_ROWS, tile)
            act[:, set_rows, cols] = (swish * pre_up).astype(BF16).reshape(shape)
            grad_gate[:, set_rows, cols] = (
                (grad_act * pre_up * (sig * (1.0 + pre_gate * (1.0 - sig)))).astype(BF16).reshape(shape)
            )
            grad_up[:, set_rows, cols] = (grad_act * swish).astype(BF16).reshape(shape)
            return carry

        lax.fori_loop(0, hidden // tile, hidden_tile, 0)

        def latent_tile(n, carry):
            cols = pl.ds(pl.multiple_of(n * wide, wide), wide)
            later = pl.ds(pl.multiple_of(latent + n * wide, wide), wide)
            shape = (peers, SET_ROWS, wide)
            out = dot(act[:, set_rows, :].reshape(count, hidden), ow_ref[:, cols])
            result_rows[:, set_rows, cols] = out.astype(BF16).reshape(shape)
            back = dot(grad_gate[:, set_rows, :].reshape(count, hidden), gw_ref[cols, :], COLS)
            back = back + dot(grad_up[:, set_rows, :].reshape(count, hidden), uw_ref[cols, :], COLS)
            result_rows[:, set_rows, later] = back.astype(BF16).reshape(shape)
            return carry

        lax.fori_loop(0, latent // wide, latent_tile, 0)

        def start(j, carry):
            back_copy(j, s).start()
            return carry

        lax.fori_loop(1, peers, start, 0)
        own_back(s).start()

    for s in range(sets):
        expert(s)

    share = hidden // groups
    all_rows = peers * sets * SET_ROWS

    def grad_copy(k):
        return pltpu.make_async_remote_copy(
            src_ref=grads_out.at[k],
            dst_ref=grads_in.at[k],
            send_sem=grad_send.at[k],
            recv_sem=grad_recv.at[k],
            device_id=group_at(k),
            device_id_type=MESH,
        )

    def weight_terms(k):
        cols = pl.ds(pl.multiple_of(lax.rem(my_group + k, groups) * share, share), share)
        rows_in = expert_rows[:, :, 0:latent].reshape(all_rows, latent)
        grad_in = expert_rows[:, :, latent:].reshape(all_rows, latent)
        gate_term = dot(rows_in, grad_gate[:, :, cols].reshape(all_rows, share), ROWS)
        up_term = dot(rows_in, grad_up[:, :, cols].reshape(all_rows, share), ROWS)
        out_term = dot(act[:, :, cols].reshape(all_rows, share), grad_in, ROWS)
        return gate_term, up_term, out_term

    def other_share(k, carry):
        gate_term, up_term, out_term = weight_terms(k)
        grads_out[k, 0:latent, 0:share] = gate_term.astype(BF16)
        grads_out[k, 0:latent, share:] = up_term.astype(BF16)
        grads_out[k, latent:, :] = out_term.astype(BF16)
        grad_copy(k).start()
        return carry

    lax.fori_loop(1, groups, other_share, 0)
    gate_grad_ref[...], up_grad_ref[...], out_grad_ref[...] = weight_terms(0)

    def combine(i):
        s, within = i // SET, i % SET
        first = s * SET_ROWS + within * MAIN
        extra = s * SET_ROWS + SET * MAIN
        shape = (peers * MAIN, latent)
        parts = []
        for part, matrix in enumerate((weigh, pick)):
            lanes = slice(part * latent, (part + 1) * latent)
            rows = jnp.concatenate(
                [
                    back_rows[:, first : first + MAIN, lanes].reshape(shape),
                    back_rows[:, extra : extra + MAIN, lanes].reshape(shape),
                ],
                axis=0,
            )
            parts.append(dot(matrix[i], rows, ROWS))
        return parts

    def ring_copy(way, step):
        lanes = pl.ds(way * latent, latent) if step == 0 else pl.ds(0, 2 * latent)
        return pltpu.make_async_remote_copy(
            src_ref=ring_out.at[way, step, :, lanes],
            dst_ref=ring_in.at[way, step, :, lanes],
            send_sem=ring_send.at[way, step],
            recv_sem=ring_recv.at[way, step],
            device_id=on_ring(-1 if way == 0 else 1),
            device_id_type=MESH,
        )

    def returned(s):
        def arrived(j, carry):
            back_copy(j, s).wait_recv()
            return carry

        lax.fori_loop(1, peers, arrived, 0)
        own_back(s).wait()

    waiting = set(range(sets))

    def ready(i):
        if i // SET in waiting:
            waiting.remove(i // SET)
            returned(i // SET)

    ready(ring - 1)
    parts = combine(ring - 1)
    for way in range(2):
        ring_out[way, 0, :, way * latent : (way + 1) * latent] = parts[way].astype(BF16)
        ring_copy(way, 0).start()
    for step in range(1, half):
        for way in range(2):
            i = 2 * (half - step) - 1 + way
            ready(i)
            parts = combine(i)
            ring_copy(way, step - 1).wait_recv()
            for part in range(2):
                lanes = slice(part * latent, (part + 1) * latent)
                value = parts[part]
                if step > 1 or part == way:
                    value = value + ring_in[way, step - 1, :, lanes].astype(F32)
                ring_out[way, step, :, lanes] = value.astype(BF16)
            ring_copy(way, step).start()
    ready(0)
    parts = combine(0)
    for way in range(2):
        ring_copy(way, half - 1).wait_recv()
    for part in range(2):
        lanes = slice(part * latent, (part + 1) * latent)
        value = parts[part]
        for way in range(2):
            if half > 1 or way == part:
                value = value + ring_in[way, half - 1, :, lanes].astype(F32)
        mid_ref[:, lanes] = value.astype(BF16)

    for k in range(1, groups):
        grad_copy(k).wait_recv()
        gate_grad_ref[...] += grads_in[k, 0:latent, 0:share].astype(F32)
        up_grad_ref[...] += grads_in[k, 0:latent, share:].astype(F32)
        out_grad_ref[...] += grads_in[k, latent:, :].astype(F32)

    for way in range(2):
        for step in range(half):
            gather_copy(way, step).wait_send()
            ring_copy(way, step).wait_send()

    def sent(j, carry):
        for s in range(sets):
            slot_copy(j, s, 0, SET_ROWS).wait_send()
            back_copy(j, s).wait_send()
        return carry

    lax.fori_loop(1, peers, sent, 0)
    for k in range(1, groups):
        grad_copy(k).wait_send()


def layer(ring, routes, gates, tokens, cotan, down, up, gate_weight, up_weight, out_weight):
    count, latent = tokens.shape[0], down.shape[1]
    hidden = gate_weight.shape[1]
    experts = lax.axis_size("expert")
    groups = lax.axis_size("dp")
    peers = experts // ring
    sets = ring // SET
    half = ring // 2
    share = hidden // groups
    chosen = 2 * peers * MAIN
    rows = sets * SET_ROWS
    vmem = pl.BlockSpec(memory_space=pltpu.VMEM)
    dma = pltpu.SemaphoreType.DMA
    return pl.pallas_call(
        partial(layer_kernel, ring),
        out_shape=(
            jax.ShapeDtypeStruct((count, 2 * latent), BF16),
            jax.ShapeDtypeStruct((latent, share), F32),
            jax.ShapeDtypeStruct((latent, share), F32),
            jax.ShapeDtypeStruct((share, latent), F32),
        ),
        in_specs=[vmem] * 9,
        out_specs=(vmem,) * 4,
        scratch_shapes=[
            pltpu.VMEM((ring, count + MAIN, 2 * latent), BF16),
            pltpu.VMEM((peers, rows, 2 * latent), BF16),
            pltpu.VMEM((peers, rows, 2 * latent), BF16),
            pltpu.VMEM((peers, rows, 2 * latent), BF16),
            pltpu.VMEM((peers, rows, 2 * latent), BF16),
            pltpu.VMEM((ring, chosen, count), BF16),
            pltpu.VMEM((ring, chosen, count), BF16),
            pltpu.VMEM((peers * MAIN, 2 * latent), F32),
            pltpu.VMEM((peers, rows, hidden), BF16),
            pltpu.VMEM((peers, rows, hidden), BF16),
            pltpu.VMEM((peers, rows, hidden), BF16),
            pltpu.VMEM((2, half, count, 2 * latent), BF16),
            pltpu.VMEM((2, half, count, 2 * latent), BF16),
            pltpu.VMEM((groups, latent + share, 2 * share), BF16),
            pltpu.VMEM((groups, latent + share, 2 * share), BF16),
            dma((2, half)),
            dma((2, half)),
            dma((sets, peers)),
            dma((sets, peers)),
            dma((sets, peers)),
            dma((sets, peers)),
            dma((2, sets)),
            dma((2, half)),
            dma((2, half)),
            dma((groups,)),
            dma((groups,)),
        ],
        compiler_params=pltpu.CompilerParams(
            collective_id=0, has_side_effects=True, vmem_limit_bytes=60 * 1024 * 1024
        ),
        name="layer",
    )(routes, gates, tokens, cotan, down, up, gate_weight, up_weight, out_weight)


def shards(
    ring,
    tokens,
    routes,
    gate_values,
    latent_down,
    gate_weight,
    up_weight,
    out_weight,
    latent_up,
    grad_mixed,
):
    latent = latent_down.shape[1]
    mid, gate_grad, up_grad, out_grad = layer(
        ring,
        routes.T,
        gate_values.T,
        tokens,
        grad_mixed,
        latent_down,
        latent_up,
        gate_weight[0],
        up_weight[0],
        out_weight[0],
    )
    combined, grad_latent = mid[:, :latent], mid[:, latent:]
    mixed = dot(combined, latent_up, COLS).astype(BF16)
    grad_tokens = dot(grad_latent, latent_down, COLS).astype(BF16)
    down_term = dot(tokens, grad_latent, ROWS).astype(BF16)
    up_term = dot(grad_mixed, combined, ROWS).astype(BF16)
    terms = jnp.concatenate([down_term, up_term], axis=1)
    terms = lax.psum_scatter(terms, "expert", scatter_dimension=0, tiled=True)
    terms = lax.psum(terms, "dp").astype(F32)
    return (
        mixed,
        grad_tokens,
        terms[:, :latent],
        terms[:, latent:],
        gate_grad[None],
        up_grad[None],
        out_grad[None],
    )


def solution(mesh, ring=RING):
    rows = P(("dp", "expert"), None)
    own = P("expert", None, None)
    return jax.shard_map(
        partial(shards, ring),
        mesh=mesh,
        in_specs=(rows, rows, rows, P(), own, own, own, P(), rows),
        out_specs=(
            rows,
            rows,
            P("expert", None),
            P("expert", None),
            P("expert", None, "dp"),
            P("expert", None, "dp"),
            P("expert", "dp", None),
        ),
        check_vma=False,
    )
```

```python
from functools import partial

import jax
import jax.numpy as jnp
from jax import lax
from jax.experimental import pallas as pl
from jax.experimental.pallas import tpu as pltpu
from jax.sharding import PartitionSpec as P

MESH = pl.DeviceIdType.MESH
ROWS = (((0,), (0,)), ((), ()))
COLS = (((1,), (1,)), ((), ()))
PLAIN = (((1,), (0,)), ((), ()))
F32 = jnp.float32
BF16 = jnp.bfloat16

RING = 8
CORES = 2
CAP = 20
MAIN = 16
EXTRA = 4
SET = 4
SET_ROWS = SET * CAP


def dot(a, b, dims=PLAIN):
    return lax.dot_general(a, b, dims, preferred_element_type=F32)


def layer_kernel(
    ring,
    routes_ref,
    gates_ref,
    tokens_ref,
    cotan_ref,
    down_ref,
    up_ref,
    gw_ref,
    uw_ref,
    ow_ref,
    mixed_ref,
    token_grad_ref,
    down_grad_ref,
    up_proj_grad_ref,
    gate_grad_ref,
    up_grad_ref,
    out_grad_ref,
    mid,
    sides,
    lates,
    x_out,
    x_in,
    x_sum,
    z_out,
    z_in,
    last_out,
    last_in,
    gathered,
    send_rows,
    expert_rows,
    result_rows,
    back_rows,
    pick,
    weigh,
    extra_sum,
    act,
    grad_gate,
    grad_up,
    ring_out,
    ring_in,
    grads_out,
    grads_in,
    gather_send,
    gather_recv,
    slot_send,
    slot_recv,
    back_send,
    back_recv,
    own_sem,
    ring_send,
    ring_recv,
    grad_send,
    grad_recv,
    side_send,
    side_recv,
    relay_send,
    late_send,
    late_recv,
    x_send,
    x_recv,
    z_send,
    z_recv,
    last_send,
    last_recv,
):
    tokens_here, latent = tokens_ref.shape[0], down_ref.shape[1]
    hidden = gw_ref.shape[1]
    experts = lax.axis_size("expert")
    groups = lax.axis_size("dp")
    columns = experts // (ring * CORES)
    peers = columns * CORES
    half = ring // 2
    sets = ring // SET
    me = lax.axis_index("expert")
    my_group = lax.axis_index("dp")
    z = lax.rem(lax.div(me, CORES), ring)
    core = lax.rem(me, CORES)
    place = lax.div(me, ring * CORES) * CORES + core

    def on_ring(step):
        other = lax.rem(z + step + ring, ring)
        return (my_group, me + (other - z) * CORES)

    def at_peer(d):
        return (my_group, (lax.div(d, CORES) * ring + z) * CORES + lax.rem(d, CORES))

    def peer(j):
        return lax.rem(place + j, peers)

    def group_at(k):
        return (lax.rem(my_group + k, groups), me)

    def mate(k, c):
        return (lax.rem(my_group + k, groups), me - core + c)

    mates = [(k, c) for k in range(1, groups) for c in range(CORES)] + [(0, 1 - core)]

    barrier = pltpu.get_barrier_semaphore()
    for step in range(1, ring):
        pl.semaphore_signal(barrier, inc=1, device_id=on_ring(step), device_id_type=MESH)
    for j in range(1, peers):
        pl.semaphore_signal(barrier, inc=1, device_id=at_peer(peer(j)), device_id_type=MESH)
    for k, c in mates:
        pl.semaphore_signal(barrier, inc=1, device_id=mate(k, c), device_id_type=MESH)

    gathered[0, 0:tokens_here, 0:latent] = dot(tokens_ref[...], down_ref[...]).astype(BF16)
    gathered[0, 0:tokens_here, latent:] = dot(cotan_ref[...], up_ref[...]).astype(BF16)
    expert_ids = lax.broadcasted_iota(jnp.int32, (experts, tokens_here), 0)
    table = jnp.zeros((experts, tokens_here), F32)
    for k in range(routes_ref.shape[0]):
        table = table + jnp.where(expert_ids == routes_ref[k : k + 1, :], gates_ref[k : k + 1, :], 0.0)
    table_high = table.astype(BF16)
    table_low = (table - table_high.astype(F32)).astype(BF16)
    per_column = ring * CORES
    for b in range(columns):
        rows = slice(b * per_column, (b + 1) * per_column)
        lanes = slice(b * tokens_here, (b + 1) * tokens_here)
        low_lanes = slice(latent + b * tokens_here, latent + (b + 1) * tokens_here)
        gathered[0, tokens_here : tokens_here + per_column, lanes] = table_high[rows, :]
        gathered[0, tokens_here : tokens_here + per_column, low_lanes] = table_low[rows, :]

    pl.semaphore_wait(barrier, (ring - 1) + (peers - 1) + len(mates))

    def gather_copy(way, step):
        target = on_ring(1 if way == 0 else -1)
        source = 0 if step == 0 else 2 * step - 1 + way
        if step < half - 1:
            src, dst = gathered.at[source], gathered.at[2 * step + 1 + way]
        else:
            lanes = pl.ds(way * latent, latent)
            src, dst = gathered.at[source, :, lanes], gathered.at[ring - 1, :, lanes]
        return pltpu.make_async_remote_copy(
            src_ref=src,
            dst_ref=dst,
            send_sem=gather_send.at[way, step],
            recv_sem=gather_recv.at[way, step],
            device_id=target,
            device_id_type=MESH,
        )

    earlier = (
        lax.broadcasted_iota(jnp.int32, (tokens_here, tokens_here), 0)
        < lax.broadcasted_iota(jnp.int32, (tokens_here, tokens_here), 1)
    ).astype(BF16)
    row_ids = lax.broadcasted_iota(jnp.int32, (per_column, tokens_here), 0)
    main_slots = lax.broadcasted_iota(jnp.int32, (MAIN, tokens_here), 0).astype(F32)

    def slot_copy(j, s, first, count):
        d = peer(j)
        rows = pl.ds(s * SET_ROWS + first, count)
        return pltpu.make_async_remote_copy(
            src_ref=send_rows.at[d, rows],
            dst_ref=expert_rows.at[place, rows],
            send_sem=slot_send.at[s, j],
            recv_sem=slot_recv.at[s, j],
            device_id=at_peer(d),
            device_id_type=MESH,
        )

    def own_slots(s, first, count):
        rows = pl.ds(s * SET_ROWS + first, count)
        return pltpu.make_async_copy(
            send_rows.at[place, rows], expert_rows.at[place, rows], own_sem.at[0, s]
        )

    def dispatch(i):
        s, within = i // SET, i % SET
        weights = []
        for b in range(columns):
            info = (
                gathered[i, tokens_here : tokens_here + per_column, b * tokens_here : (b + 1) * tokens_here].astype(F32)
                + gathered[
                    i,
                    tokens_here : tokens_here + per_column,
                    latent + b * tokens_here : latent + (b + 1) * tokens_here,
                ].astype(F32)
            )
            for c in range(CORES):
                weights.append(
                    jnp.sum(jnp.where(row_ids == z * CORES + c, info, 0.0), axis=0, keepdims=True)
                )
        weight = jnp.concatenate(weights, axis=0)
        named = weight > 0.0
        before = dot(named.astype(F32).astype(BF16), earlier)
        slot = jnp.where(named, before, -1.0)
        extra_rows = lax.broadcasted_iota(jnp.int32, (MAIN, tokens_here), 0)
        extra_slots = jnp.where(
            lax.div(extra_rows, EXTRA) == within, MAIN + lax.rem(extra_rows, EXTRA), -2
        ).astype(F32)
        hits = []
        for slots in (main_slots, extra_slots):
            for d in range(peers):
                hits.append((slots == slot[d : d + 1, :]).astype(F32))
        chosen = jnp.concatenate(hits, axis=0)
        weight_rows = jnp.concatenate(
            [jnp.broadcast_to(weight[d : d + 1, :], (MAIN, tokens_here)) for d in range(peers)], axis=0
        )
        weighted = chosen * jnp.concatenate([weight_rows, weight_rows], axis=0)
        pick[i] = chosen.astype(BF16)
        weigh[i] = weighted.astype(BF16)
        scale = jnp.sum(weighted, axis=1, keepdims=True)
        chosen = chosen.astype(BF16)
        main_count = peers * MAIN
        for part in range(2):
            lanes = slice(part * latent, (part + 1) * latent)
            rows = dot(chosen, gathered[i, 0:tokens_here, lanes])
            if part == 1:
                rows = rows * scale
            first = s * SET_ROWS + within * MAIN
            send_rows[:, first : first + MAIN, lanes] = (
                rows[:main_count].astype(BF16).reshape(peers, MAIN, latent)
            )
            extra = rows[main_count:]
            if within > 0:
                extra = extra + extra_sum[:, lanes]
            if within < SET - 1:
                extra_sum[:, lanes] = extra
            else:
                first = s * SET_ROWS + SET * MAIN
                send_rows[:, first : first + MAIN, lanes] = extra.astype(BF16).reshape(peers, MAIN, latent)
        count = MAIN if within < SET - 1 else 2 * MAIN

        def start(j, carry):
            slot_copy(j, s, within * MAIN, count).start()
            return carry

        lax.fori_loop(1, peers, start, 0)
        own_slots(s, within * MAIN, count).start()

    def side_copy(k, c, source):
        return pltpu.make_async_remote_copy(
            src_ref=source,
            dst_ref=sides.at[k, core],
            send_sem=side_send.at[k, c],
            recv_sem=side_recv.at[k, core],
            device_id=mate(k, c),
            device_id_type=MESH,
        )

    def side_arrived(k, c):
        pltpu.make_async_remote_copy(
            src_ref=tokens_ref,
            dst_ref=sides.at[k, c],
            send_sem=side_send.at[k, c],
            recv_sem=side_recv.at[k, c],
            device_id=mate(k, c),
            device_id_type=MESH,
        ).wait_recv()

    across = groups // 2

    def relay_copy(c):
        step = 1 - 2 * core
        return pltpu.make_async_remote_copy(
            src_ref=sides.at[1 + (groups - 2) * core, c],
            dst_ref=sides.at[across, c],
            send_sem=relay_send.at[c],
            recv_sem=side_recv.at[across, c],
            device_id=(lax.rem(my_group + step + groups, groups), me),
            device_id_type=MESH,
        )

    for way in range(2):
        gather_copy(way, 0).start()
    dispatch(0)
    near = sorted({1, groups - 1})
    for k in near:
        for c, source in enumerate((tokens_ref, cotan_ref)):
            side_copy(k, c, source).start()

    @pl.when(core == 0)
    def _():
        side_copy(0, 1, cotan_ref).start()

    @pl.when(core == 1)
    def _():
        side_copy(0, 0, tokens_ref).start()

    sides[0, core] = jnp.where(core == 0, tokens_ref[...], cotan_ref[...])
    for step in range(1, half):
        for way in range(2):
            gather_copy(way, step - 1).wait_recv()
            gather_copy(way, step).start()
        for way in range(2):
            dispatch(2 * step - 1 + way)
    for way in range(2):
        gather_copy(way, half - 1).wait_recv()
    dispatch(ring - 1)

    def back_copy(j, s):
        d = peer(j)
        rows = pl.ds(s * SET_ROWS, SET_ROWS)
        return pltpu.make_async_remote_copy(
            src_ref=result_rows.at[d, rows],
            dst_ref=back_rows.at[place, rows],
            send_sem=back_send.at[s, j],
            recv_sem=back_recv.at[s, j],
            device_id=at_peer(d),
            device_id_type=MESH,
        )

    def own_back(s):
        rows = pl.ds(s * SET_ROWS, SET_ROWS)
        return pltpu.make_async_copy(result_rows.at[place, rows], back_rows.at[place, rows], own_sem.at[1, s])

    tile = min(256, hidden)
    wide = min(256, latent)
    count = peers * SET_ROWS

    def expert(s):
        def arrived(j, carry):
            slot_copy(j, s, 0, SET_ROWS).wait_recv()
            return carry

        lax.fori_loop(1, peers, arrived, 0)
        own_slots(s, 0, SET_ROWS).wait()
        set_rows = slice(s * SET_ROWS, (s + 1) * SET_ROWS)

        def hidden_tile(h, carry):
            cols = pl.ds(pl.multiple_of(h * tile, tile), tile)
            rows_in = expert_rows[:, set_rows, 0:latent].reshape(count, latent)
            grad_in = expert_rows[:, set_rows, latent:].reshape(count, latent)
            pre_gate = dot(rows_in, gw_ref[:, cols])
            pre_up = dot(rows_in, uw_ref[:, cols])
            grad_act = dot(grad_in, ow_ref[cols, :], COLS)
            sig = 1.0 / (1.0 + jnp.exp(-pre_gate))
            swish = pre_gate * sig
            shape = (peers, SET_ROWS, tile)
            act[:, set_rows, cols] = (swish * pre_up).astype(BF16).reshape(shape)
            grad_gate[:, set_rows, cols] = (
                (grad_act * pre_up * (sig * (1.0 + pre_gate * (1.0 - sig)))).astype(BF16).reshape(shape)
            )
            grad_up[:, set_rows, cols] = (grad_act * swish).astype(BF16).reshape(shape)
            return carry

        lax.fori_loop(0, hidden // tile, hidden_tile, 0)

        def latent_tile(n, carry):
            cols = pl.ds(pl.multiple_of(n * wide, wide), wide)
            later = pl.ds(pl.multiple_of(latent + n * wide, wide), wide)
            shape = (peers, SET_ROWS, wide)
            out = dot(act[:, set_rows, :].reshape(count, hidden), ow_ref[:, cols])
            result_rows[:, set_rows, cols] = out.astype(BF16).reshape(shape)
            back = dot(grad_gate[:, set_rows, :].reshape(count, hidden), gw_ref[cols, :], COLS)
            back = back + dot(grad_up[:, set_rows, :].reshape(count, hidden), uw_ref[cols, :], COLS)
            result_rows[:, set_rows, later] = back.astype(BF16).reshape(shape)
            return carry

        lax.fori_loop(0, latent // wide, latent_tile, 0)

        def start(j, carry):
            back_copy(j, s).start()
            return carry

        lax.fori_loop(1, peers, start, 0)
        own_back(s).start()

    for c in range(CORES):
        for k in near:
            side_arrived(k, c)
    if across > 1:
        for c in range(CORES):
            relay_copy(c).start()

    for s in range(sets):
        expert(s)

    share = hidden // groups
    all_rows = peers * sets * SET_ROWS

    def grad_copy(k):
        return pltpu.make_async_remote_copy(
            src_ref=grads_out.at[k],
            dst_ref=grads_in.at[k],
            send_sem=grad_send.at[k],
            recv_sem=grad_recv.at[k],
            device_id=group_at(k),
            device_id_type=MESH,
        )

    def weight_terms(k):
        cols = pl.ds(pl.multiple_of(lax.rem(my_group + k, groups) * share, share), share)
        rows_in = expert_rows[:, :, 0:latent].reshape(all_rows, latent)
        grad_in = expert_rows[:, :, latent:].reshape(all_rows, latent)
        gate_term = dot(rows_in, grad_gate[:, :, cols].reshape(all_rows, share), ROWS)
        up_term = dot(rows_in, grad_up[:, :, cols].reshape(all_rows, share), ROWS)
        out_term = dot(act[:, :, cols].reshape(all_rows, share), grad_in, ROWS)
        return gate_term, up_term, out_term

    def other_share(k, carry):
        gate_term, up_term, out_term = weight_terms(k)
        grads_out[k, 0:latent, 0:share] = gate_term.astype(BF16)
        grads_out[k, 0:latent, share:] = up_term.astype(BF16)
        grads_out[k, latent:, :] = out_term.astype(BF16)
        grad_copy(k).start()
        return carry

    lax.fori_loop(1, groups, other_share, 0)
    gate_grad_ref[...], up_grad_ref[...], out_grad_ref[...] = weight_terms(0)

    def combine(i):
        s, within = i // SET, i % SET
        first = s * SET_ROWS + within * MAIN
        extra = s * SET_ROWS + SET * MAIN
        shape = (peers * MAIN, latent)
        parts = []
        for part, matrix in enumerate((weigh, pick)):
            lanes = slice(part * latent, (part + 1) * latent)
            rows = jnp.concatenate(
                [
                    back_rows[:, first : first + MAIN, lanes].reshape(shape),
                    back_rows[:, extra : extra + MAIN, lanes].reshape(shape),
                ],
                axis=0,
            )
            parts.append(dot(matrix[i], rows, ROWS))
        return parts

    def ring_copy(way, step):
        lanes = pl.ds(way * latent, latent) if step == 0 else pl.ds(0, 2 * latent)
        return pltpu.make_async_remote_copy(
            src_ref=ring_out.at[way, step, :, lanes],
            dst_ref=ring_in.at[way, step, :, lanes],
            send_sem=ring_send.at[way, step],
            recv_sem=ring_recv.at[way, step],
            device_id=on_ring(-1 if way == 0 else 1),
            device_id_type=MESH,
        )

    def returned(s):
        def arrived(j, carry):
            back_copy(j, s).wait_recv()
            return carry

        lax.fori_loop(1, peers, arrived, 0)
        own_back(s).wait()

    waiting = set(range(sets))

    def ready(i):
        if i // SET in waiting:
            waiting.remove(i // SET)
            returned(i // SET)

    ready(ring - 1)
    parts = combine(ring - 1)
    for way in range(2):
        ring_out[way, 0, :, way * latent : (way + 1) * latent] = parts[way].astype(BF16)
        ring_copy(way, 0).start()
    for step in range(1, half):
        for way in range(2):
            i = 2 * (half - step) - 1 + way
            ready(i)
            parts = combine(i)
            ring_copy(way, step - 1).wait_recv()
            for part in range(2):
                lanes = slice(part * latent, (part + 1) * latent)
                value = parts[part]
                if step > 1 or part == way:
                    value = value + ring_in[way, step - 1, :, lanes].astype(F32)
                ring_out[way, step, :, lanes] = value.astype(BF16)
            ring_copy(way, step).start()
    ready(0)
    parts = combine(0)
    for way in range(2):
        ring_copy(way, half - 1).wait_recv()
    for part in range(2):
        lanes = slice(part * latent, (part + 1) * latent)
        value = parts[part]
        for way in range(2):
            if half > 1 or way == part:
                value = value + ring_in[way, half - 1, :, lanes].astype(F32)
        mid[:, lanes] = value.astype(BF16)

    block = latent // groups
    features = tokens_ref.shape[1]
    column_rows = features // columns
    ring_rows = column_rows // ring
    last_rows = ring_rows // CORES

    def late_lanes(k, c):
        start = latent * (1 - c) + block * lax.rem(my_group + k, groups)
        return pl.ds(pl.multiple_of(start, block), block)

    def late_copy(k, c):
        return pltpu.make_async_remote_copy(
            src_ref=mid.at[:, late_lanes(k, c)],
            dst_ref=lates.at[k, core],
            send_sem=late_send.at[k, c],
            recv_sem=late_recv.at[k, core],
            device_id=mate(k, c),
            device_id_type=MESH,
        )

    def late_arrived(k, c):
        pltpu.make_async_remote_copy(
            src_ref=lates.at[k, c],
            dst_ref=lates.at[k, c],
            send_sem=late_send.at[k, c],
            recv_sem=late_recv.at[k, c],
            device_id=mate(k, c),
            device_id_type=MESH,
        ).wait_recv()

    for k, c in mates:
        late_copy(k, c).start()
    lates[0, core] = mid[:, late_lanes(0, core)]
    mixed_ref[...] = dot(mid[:, 0:latent], up_ref[...], COLS).astype(BF16)
    token_grad_ref[...] = dot(mid[:, latent:], down_ref[...], COLS).astype(BF16)

    side_arrived(0, 1 - core)
    if across > 1:
        for c in range(CORES):
            side_arrived(across, c)
    for k, c in mates:
        late_arrived(k, c)
    both = groups * CORES * tokens_here

    def term_rows(k):
        cols = pl.ds(pl.multiple_of(lax.rem(lax.div(me, ring * CORES) + k, columns) * column_rows, column_rows), column_rows)
        term = dot(lates[...].reshape(both, block), sides[:, :, :, cols].reshape(both, column_rows), ROWS)
        return term.T

    def x_copy(k):
        return pltpu.make_async_remote_copy(
            src_ref=x_out.at[k],
            dst_ref=x_in.at[k],
            send_sem=x_send.at[k],
            recv_sem=x_recv.at[k],
            device_id=at_peer(peer(k * CORES)),
            device_id_type=MESH,
        )

    for k in range(1, columns):
        x_out[k] = term_rows(k).astype(BF16)
        x_copy(k).start()
    total = term_rows(0)
    for k in range(1, columns):
        x_copy(k).wait_recv()
        total = total + x_in[k].astype(F32)
    x_sum[...] = total.reshape(ring, ring_rows, block)
    z_out[...] = x_sum[...].astype(BF16)

    def z_copy(r):
        return pltpu.make_async_remote_copy(
            src_ref=z_out.at[lax.rem(z + r, ring)],
            dst_ref=z_in.at[r],
            send_sem=z_send.at[r],
            recv_sem=z_recv.at[r],
            device_id=on_ring(r),
            device_id_type=MESH,
        )

    for r in range(1, ring):
        z_copy(r).start()
    total = x_sum[z]
    for r in range(1, ring):
        z_copy(r).wait_recv()
        total = total + z_in[r].astype(F32)
    last_out[...] = total.reshape(CORES, last_rows, block)

    def last_copy(k, c, slot):
        return pltpu.make_async_remote_copy(
            src_ref=last_out.at[c],
            dst_ref=last_in.at[k, slot],
            send_sem=last_send.at[k, c],
            recv_sem=last_recv.at[k, slot],
            device_id=mate(k, c),
            device_id_type=MESH,
        )

    for k, c in mates:
        last_copy(k, c, core).start()
    last_in[0, core] = last_out[core]

    for k in range(1, groups):
        grad_copy(k).wait_recv()
        gate_grad_ref[...] += grads_in[k, 0:latent, 0:share].astype(F32)
        up_grad_ref[...] += grads_in[k, 0:latent, share:].astype(F32)
        out_grad_ref[...] += grads_in[k, latent:, :].astype(F32)

    for k, c in mates:
        last_copy(k, c, c).wait_recv()
    for k in range(groups):
        lanes = pl.ds(pl.multiple_of(lax.rem(my_group + groups - k, groups) * block, block), block)
        down_grad_ref[:, lanes] = last_in[k, 0]
        up_proj_grad_ref[:, lanes] = last_in[k, 1]

    for k in near:
        for c in range(CORES):
            side_copy(k, c, tokens_ref).wait_send()
    side_copy(0, 1 - core, tokens_ref).wait_send()
    if across > 1:
        for c in range(CORES):
            relay_copy(c).wait_send()
    for k, c in mates:
        late_copy(k, c).wait_send()
        last_copy(k, c, core).wait_send()
    for k in range(1, columns):
        x_copy(k).wait_send()
    for r in range(1, ring):
        z_copy(r).wait_send()

    for way in range(2):
        for step in range(half):
            gather_copy(way, step).wait_send()
            ring_copy(way, step).wait_send()

    def sent(j, carry):
        for s in range(sets):
            slot_copy(j, s, 0, SET_ROWS).wait_send()
            back_copy(j, s).wait_send()
        return carry

    lax.fori_loop(1, peers, sent, 0)
    for k in range(1, groups):
        grad_copy(k).wait_send()


def layer(ring, routes, gates, tokens, cotan, down, up, gate_weight, up_weight, out_weight):
    count, latent = tokens.shape[0], down.shape[1]
    hidden = gate_weight.shape[1]
    experts = lax.axis_size("expert")
    groups = lax.axis_size("dp")
    peers = experts // ring
    sets = ring // SET
    half = ring // 2
    share = hidden // groups
    chosen = 2 * peers * MAIN
    rows = sets * SET_ROWS
    features = tokens.shape[1]
    columns = peers // CORES
    block = latent // groups
    last_rows = features // experts
    ring_rows = last_rows * CORES
    vmem = pl.BlockSpec(memory_space=pltpu.VMEM)
    dma = pltpu.SemaphoreType.DMA
    return pl.pallas_call(
        partial(layer_kernel, ring),
        out_shape=(
            jax.ShapeDtypeStruct((count, features), BF16),
            jax.ShapeDtypeStruct((count, features), BF16),
            jax.ShapeDtypeStruct((last_rows, latent), F32),
            jax.ShapeDtypeStruct((last_rows, latent), F32),
            jax.ShapeDtypeStruct((latent, share), F32),
            jax.ShapeDtypeStruct((latent, share), F32),
            jax.ShapeDtypeStruct((share, latent), F32),
        ),
        in_specs=[vmem] * 9,
        out_specs=(vmem,) * 7,
        scratch_shapes=[
            pltpu.VMEM((count, 2 * latent), BF16),
            pltpu.VMEM((groups, CORES, count, features), BF16),
            pltpu.VMEM((groups, CORES, count, block), BF16),
            pltpu.VMEM((columns, features // columns, block), BF16),
            pltpu.VMEM((columns, features // columns, block), BF16),
            pltpu.VMEM((ring, ring_rows, block), F32),
            pltpu.VMEM((ring, ring_rows, block), BF16),
            pltpu.VMEM((ring, ring_rows, block), BF16),
            pltpu.VMEM((CORES, last_rows, block), F32),
            pltpu.VMEM((groups, CORES, last_rows, block), F32),
            pltpu.VMEM((ring, count + MAIN, 2 * latent), BF16),
            pltpu.VMEM((peers, rows, 2 * latent), BF16),
            pltpu.VMEM((peers, rows, 2 * latent), BF16),
            pltpu.VMEM((peers, rows, 2 * latent), BF16),
            pltpu.VMEM((peers, rows, 2 * latent), BF16),
            pltpu.VMEM((ring, chosen, count), BF16),
            pltpu.VMEM((ring, chosen, count), BF16),
            pltpu.VMEM((peers * MAIN, 2 * latent), F32),
            pltpu.VMEM((peers, rows, hidden), BF16),
            pltpu.VMEM((peers, rows, hidden), BF16),
            pltpu.VMEM((peers, rows, hidden), BF16),
            pltpu.VMEM((2, half, count, 2 * latent), BF16),
            pltpu.VMEM((2, half, count, 2 * latent), BF16),
            pltpu.VMEM((groups, latent + share, 2 * share), BF16),
            pltpu.VMEM((groups, latent + share, 2 * share), BF16),
            dma((2, half)),
            dma((2, half)),
            dma((sets, peers)),
            dma((sets, peers)),
            dma((sets, peers)),
            dma((sets, peers)),
            dma((2, sets)),
            dma((2, half)),
            dma((2, half)),
            dma((groups,)),
            dma((groups,)),
            dma((groups, CORES)),
            dma((groups, CORES)),
            dma((CORES,)),
            dma((groups, CORES)),
            dma((groups, CORES)),
            dma((columns,)),
            dma((columns,)),
            dma((ring,)),
            dma((ring,)),
            dma((groups, CORES)),
            dma((groups, CORES)),
        ],
        compiler_params=pltpu.CompilerParams(
            collective_id=0, has_side_effects=True, vmem_limit_bytes=60 * 1024 * 1024
        ),
        name="layer",
    )(routes, gates, tokens, cotan, down, up, gate_weight, up_weight, out_weight)


def shards(
    ring,
    tokens,
    routes,
    gate_values,
    latent_down,
    gate_weight,
    up_weight,
    out_weight,
    latent_up,
    grad_mixed,
):
    mixed, grad_tokens, down_grad, up_proj_grad, gate_grad, up_grad, out_grad = layer(
        ring,
        routes.T,
        gate_values.T,
        tokens,
        grad_mixed,
        latent_down,
        latent_up,
        gate_weight[0],
        up_weight[0],
        out_weight[0],
    )
    return mixed, grad_tokens, down_grad, up_proj_grad, gate_grad[None], up_grad[None], out_grad[None]


def solution(mesh, ring=RING):
    rows = P(("dp", "expert"), None)
    own = P("expert", None, None)
    return jax.shard_map(
        partial(shards, ring),
        mesh=mesh,
        in_specs=(rows, rows, rows, P(), own, own, own, P(), rows),
        out_specs=(
            rows,
            rows,
            P("expert", None),
            P("expert", None),
            P("expert", None, "dp"),
            P("expert", None, "dp"),
            P("expert", "dp", None),
        ),
        check_vma=False,
    )
```

```python
from functools import partial

import jax
import jax.numpy as jnp
from jax import lax
from jax.experimental import pallas as pl
from jax.experimental.pallas import tpu as pltpu
from jax.sharding import PartitionSpec as P

MESH = pl.DeviceIdType.MESH
ROWS = (((0,), (0,)), ((), ()))
COLS = (((1,), (1,)), ((), ()))
PLAIN = (((1,), (0,)), ((), ()))
F32 = jnp.float32
BF16 = jnp.bfloat16

RING = 8
CORES = 2
CAP = 20
MAIN = 16
EXTRA = 4
SET = 4
SET_ROWS = SET * CAP


def dot(a, b, dims=PLAIN):
    return lax.dot_general(a, b, dims, preferred_element_type=F32)


def layer_kernel(
    ring,
    routes_ref,
    gates_ref,
    tokens_hbm,
    cotan_hbm,
    down_hbm,
    up_hbm,
    gw_hbm,
    uw_hbm,
    ow_hbm,
    mixed_hbm,
    token_grad_hbm,
    down_grad_hbm,
    up_proj_grad_hbm,
    gate_grad_hbm,
    up_grad_hbm,
    out_grad_hbm,
    tokens_ref,
    cotan_ref,
    down_ref,
    up_ref,
    gw_ref,
    uw_ref,
    ow_ref,
    mixed_ref,
    token_grad_ref,
    down_grad_ref,
    up_proj_grad_ref,
    gate_grad_ref,
    up_grad_ref,
    out_grad_ref,
    load_sem,
    store_sem,
    mid,
    sides,
    lates,
    x_out,
    x_in,
    x_sum,
    z_out,
    z_in,
    last_out,
    last_in,
    gathered,
    send_rows,
    expert_rows,
    result_rows,
    back_rows,
    pick,
    weigh,
    extra_sum,
    act,
    grad_gate,
    grad_up,
    ring_out,
    ring_in,
    grads_out,
    grads_in,
    gather_send,
    gather_recv,
    slot_send,
    slot_recv,
    back_send,
    back_recv,
    own_sem,
    ring_send,
    ring_recv,
    grad_send,
    grad_recv,
    side_send,
    side_recv,
    relay_send,
    late_send,
    late_recv,
    x_send,
    x_recv,
    z_send,
    z_recv,
    last_send,
    last_recv,
):
    tokens_here, latent = tokens_ref.shape[0], down_ref.shape[1]
    hidden = gw_ref.shape[1]
    experts = lax.axis_size("expert")
    groups = lax.axis_size("dp")
    columns = experts // (ring * CORES)
    peers = columns * CORES
    half = ring // 2
    sets = ring // SET
    me = lax.axis_index("expert")
    my_group = lax.axis_index("dp")
    z = lax.rem(lax.div(me, CORES), ring)
    core = lax.rem(me, CORES)
    place = lax.div(me, ring * CORES) * CORES + core

    def on_ring(step):
        other = lax.rem(z + step + ring, ring)
        return (my_group, me + (other - z) * CORES)

    def at_peer(d):
        return (my_group, (lax.div(d, CORES) * ring + z) * CORES + lax.rem(d, CORES))

    def peer(j):
        return lax.rem(place + j, peers)

    def group_at(k):
        return (lax.rem(my_group + k, groups), me)

    def mate(k, c):
        return (lax.rem(my_group + k, groups), me - core + c)

    mates = [(k, c) for k in range(1, groups) for c in range(CORES)] + [(0, 1 - core)]

    barrier = pltpu.get_barrier_semaphore()
    for step in range(1, ring):
        pl.semaphore_signal(barrier, inc=1, device_id=on_ring(step), device_id_type=MESH)
    for j in range(1, peers):
        pl.semaphore_signal(barrier, inc=1, device_id=at_peer(peer(j)), device_id_type=MESH)
    for k, c in mates:
        pl.semaphore_signal(barrier, inc=1, device_id=mate(k, c), device_id_type=MESH)

    loads = [
        pltpu.make_async_copy(src, dst, load_sem.at[n])
        for n, (src, dst) in enumerate(
            (
                (tokens_hbm, tokens_ref),
                (down_hbm, down_ref),
                (cotan_hbm, cotan_ref),
                (up_hbm, up_ref),
                (gw_hbm, gw_ref),
                (uw_hbm, uw_ref),
                (ow_hbm, ow_ref),
            )
        )
    ]
    stores = [
        pltpu.make_async_copy(src, dst, store_sem.at[n])
        for n, (src, dst) in enumerate(
            (
                (mixed_ref, mixed_hbm),
                (token_grad_ref, token_grad_hbm),
                (down_grad_ref, down_grad_hbm),
                (up_proj_grad_ref, up_proj_grad_hbm),
                (gate_grad_ref, gate_grad_hbm),
                (up_grad_ref, up_grad_hbm),
                (out_grad_ref, out_grad_hbm),
            )
        )
    ]
    for load in loads[:4]:
        load.start()

    expert_ids = lax.broadcasted_iota(jnp.int32, (experts, tokens_here), 0)
    table = jnp.zeros((experts, tokens_here), F32)
    for k in range(routes_ref.shape[0]):
        table = table + jnp.where(expert_ids == routes_ref[k : k + 1, :], gates_ref[k : k + 1, :], 0.0)
    table = table.astype(BF16)
    per_column = ring * CORES
    for b in range(columns):
        rows = slice(b * per_column, (b + 1) * per_column)
        lanes = slice(b * tokens_here, (b + 1) * tokens_here)
        gathered[0, tokens_here : tokens_here + per_column, lanes] = table[rows, :]

    def gather_copy(way, step, part):
        source = 0 if step == 0 else 2 * step - 1 + way
        target = 2 * step + 1 + way if step < half - 1 else ring - 1
        rows = pl.ds(0, tokens_here + MAIN if part == 0 else tokens_here)
        lanes = pl.ds(part * latent, latent)
        return pltpu.make_async_remote_copy(
            src_ref=gathered.at[source, rows, lanes],
            dst_ref=gathered.at[target, rows, lanes],
            send_sem=gather_send.at[way, step, part],
            recv_sem=gather_recv.at[way, step, part],
            device_id=on_ring(1 if way == 0 else -1),
            device_id_type=MESH,
        )

    def gather_pieces(step):
        return [(way, part) for part in range(2) for way in range(2) if step < half - 1 or part == way]

    loads[0].wait()
    loads[1].wait()
    gathered[0, 0:tokens_here, 0:latent] = dot(tokens_ref[...], down_ref[...]).astype(BF16)
    pl.semaphore_wait(barrier, (ring - 1) + (peers - 1) + len(mates))
    for way in range(2):
        gather_copy(way, 0, 0).start()
    loads[2].wait()
    loads[3].wait()
    gathered[0, 0:tokens_here, latent:] = dot(cotan_ref[...], up_ref[...]).astype(BF16)
    for way in range(2):
        gather_copy(way, 0, 1).start()
    for load in loads[4:]:
        load.start()

    earlier = (
        lax.broadcasted_iota(jnp.int32, (tokens_here, tokens_here), 0)
        < lax.broadcasted_iota(jnp.int32, (tokens_here, tokens_here), 1)
    ).astype(BF16)
    row_ids = lax.broadcasted_iota(jnp.int32, (per_column, tokens_here), 0)
    main_slots = lax.broadcasted_iota(jnp.int32, (MAIN, tokens_here), 0).astype(F32)

    def slot_copy(j, s, first, count, lanes):
        d = peer(j)
        rows = pl.ds(s * SET_ROWS + first, count)
        return pltpu.make_async_remote_copy(
            src_ref=send_rows.at[d, rows, lanes],
            dst_ref=expert_rows.at[place, rows, lanes],
            send_sem=slot_send.at[s, j],
            recv_sem=slot_recv.at[s, j],
            device_id=at_peer(d),
            device_id_type=MESH,
        )

    def own_slots(s, first, count, lanes):
        rows = pl.ds(s * SET_ROWS + first, count)
        return pltpu.make_async_copy(
            send_rows.at[place, rows, lanes], expert_rows.at[place, rows, lanes], own_sem.at[0, s]
        )

    all_lanes = pl.ds(0, 2 * latent)

    def table_rows(i):
        found = []
        for b in range(columns):
            first = b * tokens_here
            info = gathered[i, tokens_here : tokens_here + per_column, first : first + tokens_here].astype(F32)
            for c in range(CORES):
                found.append(jnp.sum(jnp.where(row_ids == z * CORES + c, info, 0.0), axis=0, keepdims=True))
        return jnp.concatenate(found, axis=0)

    main_count = peers * MAIN

    def dispatch(i, part):
        s, within = i // SET, i % SET
        lanes = slice(part * latent, (part + 1) * latent)
        if part == 0:
            named = table_rows(i) > 0.0
            before = dot(named.astype(F32).astype(BF16), earlier)
            slot = jnp.where(named, before, -1.0)
            extra_rows = lax.broadcasted_iota(jnp.int32, (MAIN, tokens_here), 0)
            extra_slots = jnp.where(
                lax.div(extra_rows, EXTRA) == within, MAIN + lax.rem(extra_rows, EXTRA), -2
            ).astype(F32)
            hits = []
            for slots in (main_slots, extra_slots):
                for d in range(peers):
                    hits.append((slots == slot[d : d + 1, :]).astype(F32))
            chosen = jnp.concatenate(hits, axis=0).astype(BF16)
            pick[i] = chosen
            rows = dot(chosen, gathered[i, 0:tokens_here, lanes])
        else:
            weight = table_rows(i)
            weight_rows = jnp.concatenate(
                [jnp.broadcast_to(weight[d : d + 1, :], (MAIN, tokens_here)) for d in range(peers)], axis=0
            )
            chosen = pick[i]
            weighted = chosen.astype(F32) * jnp.concatenate([weight_rows, weight_rows], axis=0)
            weigh[i] = weighted.astype(BF16)
            scale = jnp.sum(weighted, axis=1, keepdims=True)
            rows = dot(chosen, gathered[i, 0:tokens_here, lanes]) * scale
        first = s * SET_ROWS + within * MAIN
        send_rows[:, first : first + MAIN, lanes] = rows[:main_count].astype(BF16).reshape(peers, MAIN, latent)
        extra = rows[main_count:]
        if within > 0:
            extra = extra + extra_sum[:, lanes]
        if within < SET - 1:
            extra_sum[:, lanes] = extra
        else:
            first = s * SET_ROWS + SET * MAIN
            send_rows[:, first : first + MAIN, lanes] = extra.astype(BF16).reshape(peers, MAIN, latent)
        count = MAIN if within < SET - 1 else 2 * MAIN
        lanes = pl.ds(part * latent, latent)

        def start(j, carry):
            slot_copy(j, s, within * MAIN, count, lanes).start()
            return carry

        lax.fori_loop(1, peers, start, 0)
        own_slots(s, within * MAIN, count, lanes).start()

    def side_copy(k, c, source):
        return pltpu.make_async_remote_copy(
            src_ref=source,
            dst_ref=sides.at[k, core],
            send_sem=side_send.at[k, c],
            recv_sem=side_recv.at[k, core],
            device_id=mate(k, c),
            device_id_type=MESH,
        )

    def side_arrived(k, c):
        pltpu.make_async_remote_copy(
            src_ref=tokens_ref,
            dst_ref=sides.at[k, c],
            send_sem=side_send.at[k, c],
            recv_sem=side_recv.at[k, c],
            device_id=mate(k, c),
            device_id_type=MESH,
        ).wait_recv()

    across = groups // 2

    def relay_copy(c):
        step = 1 - 2 * core
        return pltpu.make_async_remote_copy(
            src_ref=sides.at[1 + (groups - 2) * core, c],
            dst_ref=sides.at[across, c],
            send_sem=relay_send.at[c],
            recv_sem=side_recv.at[across, c],
            device_id=(lax.rem(my_group + step + groups, groups), me),
            device_id_type=MESH,
        )

    for part in range(2):
        dispatch(0, part)
    near = sorted({1, groups - 1})
    for k in near:
        for c, source in enumerate((tokens_ref, cotan_ref)):
            side_copy(k, c, source).start()

    @pl.when(core == 0)
    def _():
        side_copy(0, 1, cotan_ref).start()

    @pl.when(core == 1)
    def _():
        side_copy(0, 0, tokens_ref).start()

    sides[0, core] = jnp.where(core == 0, tokens_ref[...], cotan_ref[...])
    for step in range(1, half):
        for part in range(2):
            for way in range(2):
                gather_copy(way, step - 1, part).wait_recv()
                if (way, part) in gather_pieces(step):
                    gather_copy(way, step, part).start()
            for way in range(2):
                dispatch(2 * step - 1 + way, part)

    back_pieces = [((SET - 1) * MAIN, 2 * MAIN)] + [(n * MAIN, MAIN) for n in range(SET - 2, -1, -1)]

    def back_copy(j, s, n):
        d = peer(j)
        first, count = back_pieces[n]
        rows = pl.ds(s * SET_ROWS + first, count)
        return pltpu.make_async_remote_copy(
            src_ref=result_rows.at[d, rows],
            dst_ref=back_rows.at[place, rows],
            send_sem=back_send.at[s, n, j],
            recv_sem=back_recv.at[s, n, j],
            device_id=at_peer(d),
            device_id_type=MESH,
        )

    def own_back(s, n):
        first, count = back_pieces[n]
        rows = pl.ds(s * SET_ROWS + first, count)
        return pltpu.make_async_copy(result_rows.at[place, rows], back_rows.at[place, rows], own_sem.at[1 + n, s])

    tile = min(256, hidden)
    wide = min(256, latent)
    count = peers * SET_ROWS

    def send_back(s, n):
        def start(j, carry):
            back_copy(j, s, n).start()
            return carry

        lax.fori_loop(1, peers, start, 0)
        own_back(s, n).start()

    left_pieces = set()

    def back_left(s, n):
        def left(j, carry):
            back_copy(j, s, n).wait_send()
            return carry

        left_pieces.add((s, n))
        lax.fori_loop(1, peers, left, 0)

    def slots_arrived(s):
        def arrived(j, carry):
            slot_copy(j, s, 0, SET_ROWS, all_lanes).wait_recv()
            return carry

        lax.fori_loop(1, peers, arrived, 0)
        own_slots(s, 0, SET_ROWS, all_lanes).wait()

    def expert(s):
        set_rows = slice(s * SET_ROWS, (s + 1) * SET_ROWS)

        def hidden_tile(h, carry):
            cols = pl.ds(pl.multiple_of(h * tile, tile), tile)
            rows_in = expert_rows[:, set_rows, 0:latent].reshape(count, latent)
            grad_in = expert_rows[:, set_rows, latent:].reshape(count, latent)
            pre_gate = dot(rows_in, gw_ref[:, cols])
            pre_up = dot(rows_in, uw_ref[:, cols])
            grad_act = dot(grad_in, ow_ref[cols, :], COLS)
            sig = 1.0 / (1.0 + jnp.exp(-pre_gate))
            swish = pre_gate * sig
            shape = (peers, SET_ROWS, tile)
            act[:, set_rows, cols] = (swish * pre_up).astype(BF16).reshape(shape)
            grad_gate[:, set_rows, cols] = (
                (grad_act * pre_up * (sig * (1.0 + pre_gate * (1.0 - sig)))).astype(BF16).reshape(shape)
            )
            grad_up[:, set_rows, cols] = (grad_act * swish).astype(BF16).reshape(shape)
            return carry

        lax.fori_loop(0, hidden // tile, hidden_tile, 0)

        def latent_tile(n, carry):
            cols = pl.ds(pl.multiple_of(n * wide, wide), wide)
            later = pl.ds(pl.multiple_of(latent + n * wide, wide), wide)
            shape = (peers, SET_ROWS, wide)
            out = dot(act[:, set_rows, :].reshape(count, hidden), ow_ref[:, cols])
            result_rows[:, set_rows, cols] = out.astype(BF16).reshape(shape)
            back = dot(grad_gate[:, set_rows, :].reshape(count, hidden), gw_ref[cols, :], COLS)
            back = back + dot(grad_up[:, set_rows, :].reshape(count, hidden), uw_ref[cols, :], COLS)
            result_rows[:, set_rows, later] = back.astype(BF16).reshape(shape)
            return carry

        lax.fori_loop(0, latent // wide, latent_tile, 0)


    for load in loads[4:]:
        load.wait()
    for s in range(sets - 1):
        slots_arrived(s)
        expert(s)
    for way, part in gather_pieces(half - 1):
        gather_copy(way, half - 1, part).wait_recv()
    for part in range(2):
        dispatch(ring - 1, part)
    for c in range(CORES):
        for k in near:
            side_arrived(k, c)
    if across > 1:
        for c in range(CORES):
            relay_copy(c).start()
    last_set = sets - 1
    slots_arrived(last_set)
    for s in range(last_set):
        send_back(s, 0)
    expert(last_set)
    send_back(last_set, 0)

    share = hidden // groups
    all_rows = peers * sets * SET_ROWS

    def grad_copy(k):
        return pltpu.make_async_remote_copy(
            src_ref=grads_out.at[k],
            dst_ref=grads_in.at[k],
            send_sem=grad_send.at[k],
            recv_sem=grad_recv.at[k],
            device_id=group_at(k),
            device_id_type=MESH,
        )

    def weight_terms(k):
        cols = pl.ds(pl.multiple_of(lax.rem(my_group + k, groups) * share, share), share)
        rows_in = expert_rows[:, :, 0:latent].reshape(all_rows, latent)
        grad_in = expert_rows[:, :, latent:].reshape(all_rows, latent)
        gate_term = dot(rows_in, grad_gate[:, :, cols].reshape(all_rows, share), ROWS)
        up_term = dot(rows_in, grad_up[:, :, cols].reshape(all_rows, share), ROWS)
        out_term = dot(act[:, :, cols].reshape(all_rows, share), grad_in, ROWS)
        return gate_term, up_term, out_term

    def other_share(k, carry):
        gate_term, up_term, out_term = weight_terms(k)
        grads_out[k, 0:latent, 0:share] = gate_term.astype(BF16)
        grads_out[k, 0:latent, share:] = up_term.astype(BF16)
        grads_out[k, latent:, :] = out_term.astype(BF16)
        grad_copy(k).start()
        return carry

    lax.fori_loop(1, groups - 1, other_share, 0)
    back_left(last_set, 0)
    send_back(last_set, 1)
    send_back(last_set, 2)
    lax.fori_loop(groups - 1, groups, other_share, 0)

    def combine(i):
        s, within = i // SET, i % SET
        first = s * SET_ROWS + within * MAIN
        extra = s * SET_ROWS + SET * MAIN
        shape = (peers * MAIN, latent)
        parts = []
        for part, matrix in enumerate((weigh, pick)):
            lanes = slice(part * latent, (part + 1) * latent)
            rows = jnp.concatenate(
                [
                    back_rows[:, first : first + MAIN, lanes].reshape(shape),
                    back_rows[:, extra : extra + MAIN, lanes].reshape(shape),
                ],
                axis=0,
            )
            parts.append(dot(matrix[i], rows, ROWS))
        return parts

    def ring_copy(way, step, part):
        lanes = pl.ds(part * latent, latent)
        return pltpu.make_async_remote_copy(
            src_ref=ring_out.at[way, step, :, lanes],
            dst_ref=ring_in.at[way, step, :, lanes],
            send_sem=ring_send.at[way, step, part],
            recv_sem=ring_recv.at[way, step, part],
            device_id=on_ring(-1 if way == 0 else 1),
            device_id_type=MESH,
        )

    def ring_pieces(step):
        pieces = [(way, 1 - way) for way in range(2)] if step > 0 else []
        return pieces + [(way, way) for way in range(2)]

    arrived_pieces = set()

    def ready(i):
        s = i // SET
        n = SET - 1 - i % SET
        if (s, n) in arrived_pieces:
            return
        arrived_pieces.add((s, n))

        def arrived(j, carry):
            back_copy(j, s, n).wait_recv()
            return carry

        lax.fori_loop(1, peers, arrived, 0)
        own_back(s, n).wait()

    ready(ring - 1)
    parts = combine(ring - 1)
    for way, part in ring_pieces(0):
        ring_out[way, 0, :, part * latent : (part + 1) * latent] = parts[part].astype(BF16)
        ring_copy(way, 0, part).start()
    gate_grad_ref[...], up_grad_ref[...], out_grad_ref[...] = weight_terms(0)
    back_left(last_set, 1)
    back_left(last_set, 2)
    send_back(last_set, 3)
    for s in range(last_set):
        for n in range(1, SET):
            send_back(s, n)
    for step in range(1, half):
        parts = []
        for way in range(2):
            i = 2 * (half - step) - 1 + way
            ready(i)
            parts.append(combine(i))
        for way, part in ring_pieces(step):
            lanes = slice(part * latent, (part + 1) * latent)
            value = parts[way][part]
            if (way, part) in ring_pieces(step - 1):
                ring_copy(way, step - 1, part).wait_recv()
                value = value + ring_in[way, step - 1, :, lanes].astype(F32)
            ring_out[way, step, :, lanes] = value.astype(BF16)
            ring_copy(way, step, part).start()
    ready(0)
    parts = combine(0)
    for part in range(2):
        lanes = slice(part * latent, (part + 1) * latent)
        value = parts[part]
        for way in range(2):
            if (way, part) in ring_pieces(half - 1):
                ring_copy(way, half - 1, part).wait_recv()
                value = value + ring_in[way, half - 1, :, lanes].astype(F32)
        mid[:, lanes] = value.astype(BF16)

    block = latent // groups
    features = tokens_ref.shape[1]
    column_rows = features // columns
    ring_rows = column_rows // ring
    last_rows = ring_rows // CORES

    def late_lanes(k, c):
        start = latent * (1 - c) + block * lax.rem(my_group + k, groups)
        return pl.ds(pl.multiple_of(start, block), block)

    def late_copy(k, c):
        return pltpu.make_async_remote_copy(
            src_ref=mid.at[:, late_lanes(k, c)],
            dst_ref=lates.at[k, core],
            send_sem=late_send.at[k, c],
            recv_sem=late_recv.at[k, core],
            device_id=mate(k, c),
            device_id_type=MESH,
        )

    def late_arrived(k, c):
        pltpu.make_async_remote_copy(
            src_ref=lates.at[k, c],
            dst_ref=lates.at[k, c],
            send_sem=late_send.at[k, c],
            recv_sem=late_recv.at[k, c],
            device_id=mate(k, c),
            device_id_type=MESH,
        ).wait_recv()

    for k, c in mates:
        late_copy(k, c).start()
    lates[0, core] = mid[:, late_lanes(0, core)]
    mixed_ref[...] = dot(mid[:, 0:latent], up_ref[...], COLS)
    token_grad_ref[...] = dot(mid[:, latent:], down_ref[...], COLS)
    stores[0].start()
    stores[1].start()

    side_arrived(0, 1 - core)
    if across > 1:
        for c in range(CORES):
            side_arrived(across, c)
    for k, c in mates:
        late_arrived(k, c)
    both = groups * CORES * tokens_here
    late_columns = lates[...].reshape(both, block).astype(F32).T.astype(BF16)

    def term_rows(k):
        cols = pl.ds(pl.multiple_of(lax.rem(lax.div(me, ring * CORES) + k, columns) * column_rows, column_rows), column_rows)
        return dot(late_columns, sides[:, :, :, cols].reshape(both, column_rows)).T

    def x_copy(k):
        return pltpu.make_async_remote_copy(
            src_ref=x_out.at[k],
            dst_ref=x_in.at[k],
            send_sem=x_send.at[k],
            recv_sem=x_recv.at[k],
            device_id=at_peer(peer(k * CORES)),
            device_id_type=MESH,
        )

    for k in range(1, columns):
        x_out[k] = term_rows(k).astype(BF16)
        x_copy(k).start()
    total = term_rows(0)
    for k in range(1, groups):
        grad_copy(k).wait_recv()
        gate_grad_ref[...] += grads_in[k, 0:latent, 0:share].astype(F32)
        up_grad_ref[...] += grads_in[k, 0:latent, share:].astype(F32)
        out_grad_ref[...] += grads_in[k, latent:, :].astype(F32)
    for store in stores[4:]:
        store.start()
    for k in range(1, columns):
        x_copy(k).wait_recv()
        total = total + x_in[k].astype(F32)
    x_sum[...] = total.reshape(ring, ring_rows, block)
    z_out[...] = x_sum[...].astype(BF16)

    def z_copy(r):
        return pltpu.make_async_remote_copy(
            src_ref=z_out.at[lax.rem(z + r, ring)],
            dst_ref=z_in.at[r],
            send_sem=z_send.at[r],
            recv_sem=z_recv.at[r],
            device_id=on_ring(r),
            device_id_type=MESH,
        )

    for r in range(1, ring):
        z_copy(r).start()
    total = x_sum[z]
    for r in range(1, ring):
        z_copy(r).wait_recv()
        total = total + z_in[r].astype(F32)
    last_out[...] = total.reshape(CORES, last_rows, block)

    def last_copy(k, c, slot):
        return pltpu.make_async_remote_copy(
            src_ref=last_out.at[c],
            dst_ref=last_in.at[k, slot],
            send_sem=last_send.at[k, c],
            recv_sem=last_recv.at[k, slot],
            device_id=mate(k, c),
            device_id_type=MESH,
        )

    for k, c in mates:
        last_copy(k, c, core).start()
    last_in[0, core] = last_out[core]

    for k, c in mates:
        last_copy(k, c, c).wait_recv()
    for k in range(groups):
        lanes = pl.ds(pl.multiple_of(lax.rem(my_group + groups - k, groups) * block, block), block)
        down_grad_ref[:, lanes] = last_in[k, 0]
        up_proj_grad_ref[:, lanes] = last_in[k, 1]
    stores[2].start()
    stores[3].start()

    for k in near:
        for c in range(CORES):
            side_copy(k, c, tokens_ref).wait_send()
    side_copy(0, 1 - core, tokens_ref).wait_send()
    if across > 1:
        for c in range(CORES):
            relay_copy(c).wait_send()
    for k, c in mates:
        late_copy(k, c).wait_send()
        last_copy(k, c, core).wait_send()
    for k in range(1, columns):
        x_copy(k).wait_send()
    for r in range(1, ring):
        z_copy(r).wait_send()

    for step in range(half):
        for way, part in gather_pieces(step):
            gather_copy(way, step, part).wait_send()
        for way, part in ring_pieces(step):
            ring_copy(way, step, part).wait_send()

    def sent(j, carry):
        for s in range(sets):
            slot_copy(j, s, 0, SET_ROWS, all_lanes).wait_send()
            for n in range(SET):
                if (s, n) not in left_pieces:
                    back_copy(j, s, n).wait_send()
        return carry

    lax.fori_loop(1, peers, sent, 0)
    for k in range(1, groups):
        grad_copy(k).wait_send()
    for store in stores:
        store.wait()


def layer(ring, routes, gates, tokens, cotan, down, up, gate_weight, up_weight, out_weight):
    count, latent = tokens.shape[0], down.shape[1]
    hidden = gate_weight.shape[1]
    experts = lax.axis_size("expert")
    groups = lax.axis_size("dp")
    peers = experts // ring
    sets = ring // SET
    half = ring // 2
    share = hidden // groups
    chosen = 2 * peers * MAIN
    rows = sets * SET_ROWS
    features = tokens.shape[1]
    columns = peers // CORES
    block = latent // groups
    last_rows = features // experts
    ring_rows = last_rows * CORES
    vmem = pl.BlockSpec(memory_space=pltpu.VMEM)
    anywhere = pl.BlockSpec(memory_space=pl.ANY)
    dma = pltpu.SemaphoreType.DMA
    arrays = (tokens, cotan, down, up, gate_weight, up_weight, out_weight)
    results = (
        jax.ShapeDtypeStruct((count, features), F32),
        jax.ShapeDtypeStruct((count, features), F32),
        jax.ShapeDtypeStruct((last_rows, latent), F32),
        jax.ShapeDtypeStruct((last_rows, latent), F32),
        jax.ShapeDtypeStruct((latent, share), F32),
        jax.ShapeDtypeStruct((latent, share), F32),
        jax.ShapeDtypeStruct((share, latent), F32),
    )
    return pl.pallas_call(
        partial(layer_kernel, ring),
        out_shape=results,
        in_specs=[vmem] * 2 + [anywhere] * 7,
        out_specs=(anywhere,) * 7,
        scratch_shapes=[pltpu.VMEM(a.shape, a.dtype) for a in arrays + results]
        + [
            dma((len(arrays),)),
            dma((len(results),)),
            pltpu.VMEM((count, 2 * latent), BF16),
            pltpu.VMEM((groups, CORES, count, features), BF16),
            pltpu.VMEM((groups, CORES, count, block), BF16),
            pltpu.VMEM((columns, features // columns, block), BF16),
            pltpu.VMEM((columns, features // columns, block), BF16),
            pltpu.VMEM((ring, ring_rows, block), F32),
            pltpu.VMEM((ring, ring_rows, block), BF16),
            pltpu.VMEM((ring, ring_rows, block), BF16),
            pltpu.VMEM((CORES, last_rows, block), F32),
            pltpu.VMEM((groups, CORES, last_rows, block), F32),
            pltpu.VMEM((ring, count + MAIN, 2 * latent), BF16),
            pltpu.VMEM((peers, rows, 2 * latent), BF16),
            pltpu.VMEM((peers, rows, 2 * latent), BF16),
            pltpu.VMEM((peers, rows, 2 * latent), BF16),
            pltpu.VMEM((peers, rows, 2 * latent), BF16),
            pltpu.VMEM((ring, chosen, count), BF16),
            pltpu.VMEM((ring, chosen, count), BF16),
            pltpu.VMEM((peers * MAIN, 2 * latent), F32),
            pltpu.VMEM((peers, rows, hidden), BF16),
            pltpu.VMEM((peers, rows, hidden), BF16),
            pltpu.VMEM((peers, rows, hidden), BF16),
            pltpu.VMEM((2, half, count, 2 * latent), BF16),
            pltpu.VMEM((2, half, count, 2 * latent), BF16),
            pltpu.VMEM((groups, latent + share, 2 * share), BF16),
            pltpu.VMEM((groups, latent + share, 2 * share), BF16),
            dma((2, half, 2)),
            dma((2, half, 2)),
            dma((sets, peers)),
            dma((sets, peers)),
            dma((sets, SET, peers)),
            dma((sets, SET, peers)),
            dma((1 + SET, sets)),
            dma((2, half, 2)),
            dma((2, half, 2)),
            dma((groups,)),
            dma((groups,)),
            dma((groups, CORES)),
            dma((groups, CORES)),
            dma((CORES,)),
            dma((groups, CORES)),
            dma((groups, CORES)),
            dma((columns,)),
            dma((columns,)),
            dma((ring,)),
            dma((ring,)),
            dma((groups, CORES)),
            dma((groups, CORES)),
        ],
        compiler_params=pltpu.CompilerParams(
            collective_id=0, has_side_effects=True, vmem_limit_bytes=60 * 1024 * 1024
        ),
        name="layer",
    )(routes, gates, tokens, cotan, down, up, gate_weight, up_weight, out_weight)


def shards(
    ring,
    tokens,
    routes,
    gate_values,
    latent_down,
    gate_weight,
    up_weight,
    out_weight,
    latent_up,
    grad_mixed,
):
    mixed, grad_tokens, down_grad, up_proj_grad, gate_grad, up_grad, out_grad = layer(
        ring,
        routes.T,
        gate_values.T,
        tokens,
        grad_mixed,
        latent_down,
        latent_up,
        gate_weight[0],
        up_weight[0],
        out_weight[0],
    )
    mixed, grad_tokens = mixed.astype(BF16), grad_tokens.astype(BF16)
    return mixed, grad_tokens, down_grad, up_proj_grad, gate_grad[None], up_grad[None], out_grad[None]


def solution(mesh, ring=RING):
    rows = P(("dp", "expert"), None)
    own = P("expert", None, None)
    return jax.shard_map(
        partial(shards, ring),
        mesh=mesh,
        in_specs=(rows, rows, rows, P(), own, own, own, P(), rows),
        out_specs=(
            rows,
            rows,
            P("expert", None),
            P("expert", None),
            P("expert", None, "dp"),
            P("expert", None, "dp"),
            P("expert", "dp", None),
        ),
        check_vma=False,
    )
```

```python
from functools import partial

import jax
import jax.numpy as jnp
from jax import lax
from jax.experimental import pallas as pl
from jax.experimental.pallas import tpu as pltpu
from jax.sharding import PartitionSpec as P

MESH = pl.DeviceIdType.MESH
ROWS = (((0,), (0,)), ((), ()))
COLS = (((1,), (1,)), ((), ()))
PLAIN = (((1,), (0,)), ((), ()))
F32 = jnp.float32
BF16 = jnp.bfloat16

RING = 8
CORES = 2
CAP = 20
MAIN = 16
EXTRA = 4
SET = 4
SET_ROWS = SET * CAP


def dot(a, b, dims=PLAIN):
    return lax.dot_general(a, b, dims, preferred_element_type=F32)


def layer_kernel(
    ring,
    routes_ref,
    gates_ref,
    tokens_hbm,
    cotan_hbm,
    down_hbm,
    up_hbm,
    gw_hbm,
    uw_hbm,
    ow_hbm,
    mixed_hbm,
    token_grad_hbm,
    proj_hbm,
    gate_grad_hbm,
    up_grad_hbm,
    out_grad_hbm,
    tokens_ref,
    cotan_ref,
    down_ref,
    up_ref,
    gw_ref,
    uw_ref,
    ow_ref,
    mixed_ref,
    token_grad_ref,
    gate_grad_ref,
    up_grad_ref,
    out_grad_ref,
    load_sem,
    store_sem,
    mid,
    sides,
    lates,
    x_out,
    x_in,
    x_sum,
    z_out,
    z_in,
    last_out,
    gathered,
    send_rows,
    expert_rows,
    result_rows,
    back_rows,
    pick,
    weigh,
    extra_sum,
    act,
    grad_gate,
    grad_up,
    ring_out,
    ring_in,
    grads_out,
    grads_in,
    grads_half,
    gather_send,
    gather_recv,
    slot_send,
    slot_recv,
    back_send,
    back_recv,
    own_sem,
    ring_send,
    ring_recv,
    grad_send,
    grad_recv,
    half_send,
    half_recv,
    side_send,
    side_recv,
    relay_send,
    late_send,
    late_recv,
    x_send,
    x_recv,
    z_send,
    z_recv,
    last_send,
    last_recv,
):
    tokens_here, latent = tokens_ref.shape[0], down_ref.shape[1]
    hidden = gw_ref.shape[1]
    experts = lax.axis_size("expert")
    groups = lax.axis_size("dp")
    columns = experts // (ring * CORES)
    peers = columns * CORES
    half = ring // 2
    sets = ring // SET
    me = lax.axis_index("expert")
    my_group = lax.axis_index("dp")
    z = lax.rem(lax.div(me, CORES), ring)
    core = lax.rem(me, CORES)
    place = lax.div(me, ring * CORES) * CORES + core

    def on_ring(step):
        other = lax.rem(z + step + ring, ring)
        return (my_group, me + (other - z) * CORES)

    def at_peer(d):
        return (my_group, (lax.div(d, CORES) * ring + z) * CORES + lax.rem(d, CORES))

    def peer(j):
        return lax.rem(place + j, peers)

    def group_at(k):
        return (lax.rem(my_group + k, groups), me)

    def mate(k, c):
        return (lax.rem(my_group + k, groups), me - core + c)

    mates = [(k, c) for k in range(1, groups) for c in range(CORES)] + [(0, 1 - core)]

    barrier = pltpu.get_barrier_semaphore()
    for step in range(1, ring):
        pl.semaphore_signal(barrier, inc=1, device_id=on_ring(step), device_id_type=MESH)
    for j in range(1, peers):
        pl.semaphore_signal(barrier, inc=1, device_id=at_peer(peer(j)), device_id_type=MESH)
    for k, c in mates:
        pl.semaphore_signal(barrier, inc=1, device_id=mate(k, c), device_id_type=MESH)

    loads = [
        pltpu.make_async_copy(src, dst, load_sem.at[n])
        for n, (src, dst) in enumerate(
            (
                (tokens_hbm, tokens_ref),
                (down_hbm, down_ref),
                (cotan_hbm, cotan_ref),
                (up_hbm, up_ref),
                (gw_hbm, gw_ref),
                (uw_hbm, uw_ref),
                (ow_hbm, ow_ref),
            )
        )
    ]
    stores = [
        pltpu.make_async_copy(src, dst, store_sem.at[n])
        for n, (src, dst) in enumerate(
            (
                (mixed_ref, mixed_hbm),
                (token_grad_ref, token_grad_hbm),
                (gate_grad_ref, gate_grad_hbm),
                (up_grad_ref, up_grad_hbm),
                (out_grad_ref, out_grad_hbm),
            )
        )
    ]
    for load in loads[:2]:
        load.start()

    expert_ids = lax.broadcasted_iota(jnp.int32, (experts, tokens_here), 0)
    table = jnp.zeros((experts, tokens_here), F32)
    for k in range(routes_ref.shape[0]):
        table = table + jnp.where(expert_ids == routes_ref[k : k + 1, :], gates_ref[k : k + 1, :], 0.0)
    table = table.astype(BF16)
    per_column = ring * CORES
    for b in range(columns):
        rows = slice(b * per_column, (b + 1) * per_column)
        lanes = slice(b * tokens_here, (b + 1) * tokens_here)
        gathered[0, tokens_here : tokens_here + per_column, lanes] = table[rows, :]

    def gather_copy(way, step, part):
        source = 0 if step == 0 else 2 * step - 1 + way
        target = 2 * step + 1 + way if step < half - 1 else ring - 1
        rows = pl.ds(0, tokens_here + MAIN if part == 0 else tokens_here)
        lanes = pl.ds(part * latent, latent)
        return pltpu.make_async_remote_copy(
            src_ref=gathered.at[source, rows, lanes],
            dst_ref=gathered.at[target, rows, lanes],
            send_sem=gather_send.at[way, step, part],
            recv_sem=gather_recv.at[way, step, part],
            device_id=on_ring(1 if way == 0 else -1),
            device_id_type=MESH,
        )

    def gather_pieces(step):
        return [(way, part) for part in range(2) for way in range(2) if step < half - 1 or part == way]

    loads[0].wait()
    loads[1].wait()
    for load in loads[2:4]:
        load.start()
    gathered[0, 0:tokens_here, 0:latent] = dot(tokens_ref[...], down_ref[...]).astype(BF16)
    pl.semaphore_wait(barrier, (ring - 1) + (peers - 1) + len(mates))
    for way in range(2):
        gather_copy(way, 0, 0).start()
    loads[2].wait()
    loads[3].wait()
    gathered[0, 0:tokens_here, latent:] = dot(cotan_ref[...], up_ref[...]).astype(BF16)
    for way in range(2):
        gather_copy(way, 0, 1).start()
    for load in loads[4:]:
        load.start()

    earlier = (
        lax.broadcasted_iota(jnp.int32, (tokens_here, tokens_here), 0)
        < lax.broadcasted_iota(jnp.int32, (tokens_here, tokens_here), 1)
    ).astype(BF16)
    row_ids = lax.broadcasted_iota(jnp.int32, (per_column, tokens_here), 0)
    main_slots = lax.broadcasted_iota(jnp.int32, (MAIN, tokens_here), 0).astype(F32)

    last_set = sets - 1
    near_rows = (SET - 1) * MAIN
    chunks = [(s * SET_ROWS, SET_ROWS) for s in range(last_set)] + [
        (last_set * SET_ROWS, near_rows),
        (last_set * SET_ROWS + near_rows, SET_ROWS - near_rows),
    ]

    def chunk_of(i):
        return i // SET + (1 if i == ring - 1 else 0)

    def slot_copy(j, chunk, first, count, lanes):
        d = peer(j)
        rows = pl.ds(first, count)
        return pltpu.make_async_remote_copy(
            src_ref=send_rows.at[d, rows, lanes],
            dst_ref=expert_rows.at[place, rows, lanes],
            send_sem=slot_send.at[chunk, j],
            recv_sem=slot_recv.at[chunk, j],
            device_id=at_peer(d),
            device_id_type=MESH,
        )

    def own_slots(chunk, first, count, lanes):
        rows = pl.ds(first, count)
        return pltpu.make_async_copy(
            send_rows.at[place, rows, lanes], expert_rows.at[place, rows, lanes], own_sem.at[0, chunk]
        )

    all_lanes = pl.ds(0, 2 * latent)

    def table_rows(i):
        found = []
        for b in range(columns):
            first = b * tokens_here
            info = gathered[i, tokens_here : tokens_here + per_column, first : first + tokens_here].astype(F32)
            for c in range(CORES):
                found.append(jnp.sum(jnp.where(row_ids == z * CORES + c, info, 0.0), axis=0, keepdims=True))
        return jnp.concatenate(found, axis=0)

    main_count = peers * MAIN

    def dispatch(i, part):
        s, within = i // SET, i % SET
        lanes = slice(part * latent, (part + 1) * latent)
        if part == 0:
            named = table_rows(i) > 0.0
            before = dot(named.astype(F32).astype(BF16), earlier)
            slot = jnp.where(named, before, -1.0)
            extra_rows = lax.broadcasted_iota(jnp.int32, (MAIN, tokens_here), 0)
            extra_slots = jnp.where(
                lax.div(extra_rows, EXTRA) == within, MAIN + lax.rem(extra_rows, EXTRA), -2
            ).astype(F32)
            hits = []
            for slots in (main_slots, extra_slots):
                for d in range(peers):
                    hits.append((slots == slot[d : d + 1, :]).astype(F32))
            chosen = jnp.concatenate(hits, axis=0).astype(BF16)
            pick[i] = chosen
            rows = dot(chosen, gathered[i, 0:tokens_here, lanes])
        else:
            weight = table_rows(i)
            weight_rows = jnp.concatenate(
                [jnp.broadcast_to(weight[d : d + 1, :], (MAIN, tokens_here)) for d in range(peers)], axis=0
            )
            chosen = pick[i]
            weighted = chosen.astype(F32) * jnp.concatenate([weight_rows, weight_rows], axis=0)
            weigh[i] = weighted.astype(BF16)
            scale = jnp.sum(weighted, axis=1, keepdims=True)
            rows = dot(chosen, gathered[i, 0:tokens_here, lanes]) * scale
        first = s * SET_ROWS + within * MAIN
        send_rows[:, first : first + MAIN, lanes] = rows[:main_count].astype(BF16).reshape(peers, MAIN, latent)
        extra = rows[main_count:]
        if within > 0:
            extra = extra + extra_sum[:, lanes]
        if within < SET - 1:
            extra_sum[:, lanes] = extra
        else:
            first = s * SET_ROWS + SET * MAIN
            send_rows[:, first : first + MAIN, lanes] = extra.astype(BF16).reshape(peers, MAIN, latent)
        count = MAIN if within < SET - 1 else 2 * MAIN
        lanes = pl.ds(part * latent, latent)

        def start(j, carry):
            slot_copy(j, chunk_of(i), s * SET_ROWS + within * MAIN, count, lanes).start()
            return carry

        lax.fori_loop(1, peers, start, 0)
        own_slots(chunk_of(i), s * SET_ROWS + within * MAIN, count, lanes).start()

    def side_copy(k, c, source):
        return pltpu.make_async_remote_copy(
            src_ref=source,
            dst_ref=sides.at[k, core],
            send_sem=side_send.at[k, c],
            recv_sem=side_recv.at[k, core],
            device_id=mate(k, c),
            device_id_type=MESH,
        )

    def side_arrived(k, c):
        pltpu.make_async_remote_copy(
            src_ref=tokens_ref,
            dst_ref=sides.at[k, c],
            send_sem=side_send.at[k, c],
            recv_sem=side_recv.at[k, c],
            device_id=mate(k, c),
            device_id_type=MESH,
        ).wait_recv()

    across = groups // 2

    def relay_copy(c):
        step = 1 - 2 * core
        return pltpu.make_async_remote_copy(
            src_ref=sides.at[1 + (groups - 2) * core, c],
            dst_ref=sides.at[across, c],
            send_sem=relay_send.at[c],
            recv_sem=side_recv.at[across, c],
            device_id=(lax.rem(my_group + step + groups, groups), me),
            device_id_type=MESH,
        )

    for part in range(2):
        dispatch(0, part)
    near = sorted({1, groups - 1})
    for k in near:
        for c, source in enumerate((tokens_ref, cotan_ref)):
            side_copy(k, c, source).start()

    @pl.when(core == 0)
    def _():
        side_copy(0, 1, cotan_ref).start()

    @pl.when(core == 1)
    def _():
        side_copy(0, 0, tokens_ref).start()

    sides[0, core] = jnp.where(core == 0, tokens_ref[...], cotan_ref[...])
    for step in range(1, half):
        for part in range(2):
            for way in range(2):
                gather_copy(way, step - 1, part).wait_recv()
                if (way, part) in gather_pieces(step):
                    gather_copy(way, step, part).start()
            for way in range(2):
                dispatch(2 * step - 1 + way, part)

    back_pieces = [((SET - 1) * MAIN, 2 * MAIN)] + [(n * MAIN, MAIN) for n in range(SET - 2, -1, -1)]

    def back_copy(j, s, n):
        d = peer(j)
        first, count = back_pieces[n]
        rows = pl.ds(s * SET_ROWS + first, count)
        return pltpu.make_async_remote_copy(
            src_ref=result_rows.at[d, rows],
            dst_ref=back_rows.at[place, rows],
            send_sem=back_send.at[s, n, j],
            recv_sem=back_recv.at[s, n, j],
            device_id=at_peer(d),
            device_id_type=MESH,
        )

    def own_back(s, n):
        first, count = back_pieces[n]
        rows = pl.ds(s * SET_ROWS + first, count)
        return pltpu.make_async_copy(result_rows.at[place, rows], back_rows.at[place, rows], own_sem.at[1 + n, s])

    tile = min(256, hidden)
    wide = min(256, latent)
    def send_back(s, n):
        def start(j, carry):
            back_copy(j, s, n).start()
            return carry

        lax.fori_loop(1, peers, start, 0)
        own_back(s, n).start()

    def slots_arrived(chunk):
        def arrived(j, carry):
            slot_copy(j, chunk, *chunks[chunk], all_lanes).wait_recv()
            return carry

        lax.fori_loop(1, peers, arrived, 0)
        own_slots(chunk, *chunks[chunk], all_lanes).wait()

    def expert(chunk):
        first, per_peer = chunks[chunk]
        set_rows = slice(first, first + per_peer)
        count = peers * per_peer

        def hidden_tile(h, carry):
            cols = pl.ds(pl.multiple_of(h * tile, tile), tile)
            rows_in = expert_rows[:, set_rows, 0:latent].reshape(count, latent)
            grad_in = expert_rows[:, set_rows, latent:].reshape(count, latent)
            pre_gate = dot(rows_in, gw_ref[:, cols])
            pre_up = dot(rows_in, uw_ref[:, cols])
            grad_act = dot(grad_in, ow_ref[cols, :], COLS)
            sig = 1.0 / (1.0 + jnp.exp(-pre_gate))
            swish = pre_gate * sig
            shape = (peers, per_peer, tile)
            act[:, set_rows, cols] = (swish * pre_up).astype(BF16).reshape(shape)
            grad_gate[:, set_rows, cols] = (
                (grad_act * pre_up * (sig * (1.0 + pre_gate * (1.0 - sig)))).astype(BF16).reshape(shape)
            )
            grad_up[:, set_rows, cols] = (grad_act * swish).astype(BF16).reshape(shape)
            return carry

        lax.fori_loop(0, hidden // tile, hidden_tile, 0)

        def latent_tile(n, carry):
            cols = pl.ds(pl.multiple_of(n * wide, wide), wide)
            later = pl.ds(pl.multiple_of(latent + n * wide, wide), wide)
            shape = (peers, per_peer, wide)
            out = dot(act[:, set_rows, :].reshape(count, hidden), ow_ref[:, cols])
            result_rows[:, set_rows, cols] = out.astype(BF16).reshape(shape)
            back = dot(grad_gate[:, set_rows, :].reshape(count, hidden), gw_ref[cols, :], COLS)
            back = back + dot(grad_up[:, set_rows, :].reshape(count, hidden), uw_ref[cols, :], COLS)
            result_rows[:, set_rows, later] = back.astype(BF16).reshape(shape)
            return carry

        lax.fori_loop(0, latent // wide, latent_tile, 0)


    for load in loads[4:]:
        load.wait()
    for chunk in range(last_set):
        slots_arrived(chunk)
        expert(chunk)
    for way, part in gather_pieces(half - 1):
        gather_copy(way, half - 1, part).wait_recv()
    for part in range(2):
        dispatch(ring - 1, part)
    slots_arrived(last_set)
    expert(last_set)
    for c in range(CORES):
        for k in near:
            side_arrived(k, c)
    if across > 1:
        for c in range(CORES):
            relay_copy(c).start()
    slots_arrived(last_set + 1)
    for s in range(last_set):
        send_back(s, 0)
    expert(last_set + 1)
    send_back(last_set, 0)

    share = hidden // groups
    all_rows = peers * sets * SET_ROWS

    def grad_copy(k):
        return pltpu.make_async_remote_copy(
            src_ref=grads_out.at[k],
            dst_ref=grads_in.at[k],
            send_sem=grad_send.at[k],
            recv_sem=grad_recv.at[k],
            device_id=group_at(k),
            device_id_type=MESH,
        )

    def weight_terms(k):
        cols = pl.ds(pl.multiple_of(lax.rem(my_group + k, groups) * share, share), share)
        rows_in = expert_rows[:, :, 0:latent].reshape(all_rows, latent)
        grad_in = expert_rows[:, :, latent:].reshape(all_rows, latent)
        gate_term = dot(rows_in, grad_gate[:, :, cols].reshape(all_rows, share), ROWS)
        up_term = dot(rows_in, grad_up[:, :, cols].reshape(all_rows, share), ROWS)
        out_term = dot(act[:, :, cols].reshape(all_rows, share), grad_in, ROWS)
        return gate_term, up_term, out_term

    def other_share(k, carry):
        gate_term, up_term, out_term = weight_terms(k)
        grads_out[k, 0:latent, 0:share] = gate_term.astype(BF16)
        grads_out[k, 0:latent, share:] = up_term.astype(BF16)
        grads_out[k, latent:, :] = out_term.astype(BF16)
        return carry

    half_rows = (latent + share) // 2

    def pass_copy(way):
        return pltpu.make_async_remote_copy(
            src_ref=grads_out.at[across, pl.ds(way * half_rows, half_rows)],
            dst_ref=grads_half.at[way],
            send_sem=half_send.at[way],
            recv_sem=half_recv.at[way],
            device_id=group_at(near[way]),
            device_id_type=MESH,
        )

    if across > 1:
        lax.fori_loop(across, across + 1, other_share, 0)
        for way in range(2):
            pass_copy(way).start()
    send_back(last_set, 1)
    send_back(last_set, 2)
    lax.fori_loop(0, len(near), lambda n, carry: other_share(1 + (groups - 2) * n, carry), 0)

    def combine(i):
        s, within = i // SET, i % SET
        first = s * SET_ROWS + within * MAIN
        extra = s * SET_ROWS + SET * MAIN
        shape = (peers * MAIN, latent)
        parts = []
        for part, matrix in enumerate((weigh, pick)):
            lanes = slice(part * latent, (part + 1) * latent)
            rows = jnp.concatenate(
                [
                    back_rows[:, first : first + MAIN, lanes].reshape(shape),
                    back_rows[:, extra : extra + MAIN, lanes].reshape(shape),
                ],
                axis=0,
            )
            parts.append(dot(matrix[i], rows, ROWS))
        return parts

    def ring_copy(way, step, part):
        lanes = pl.ds(part * latent, latent)
        return pltpu.make_async_remote_copy(
            src_ref=ring_out.at[way, step, :, lanes],
            dst_ref=ring_in.at[way, step, :, lanes],
            send_sem=ring_send.at[way, step, part],
            recv_sem=ring_recv.at[way, step, part],
            device_id=on_ring(-1 if way == 0 else 1),
            device_id_type=MESH,
        )

    def ring_pieces(step):
        pieces = [(way, 1 - way) for way in range(2)] if step > 0 else []
        return pieces + [(way, way) for way in range(2)]

    arrived_pieces = set()

    def ready(i):
        s = i // SET
        n = SET - 1 - i % SET
        if (s, n) in arrived_pieces:
            return
        arrived_pieces.add((s, n))

        def arrived(j, carry):
            back_copy(j, s, n).wait_recv()
            return carry

        lax.fori_loop(1, peers, arrived, 0)
        own_back(s, n).wait()

    ready(ring - 1)
    parts = combine(ring - 1)
    for way, part in ring_pieces(0):
        ring_out[way, 0, :, part * latent : (part + 1) * latent] = parts[part].astype(BF16)
        ring_copy(way, 0, part).start()
    gate_grad_ref[...], up_grad_ref[...], out_grad_ref[...] = weight_terms(0)
    for way, k in enumerate(near):
        if across > 1:
            pass_copy(way).wait_recv()
            rows = slice(way * half_rows, (way + 1) * half_rows)
            grads_out[k, rows, :] = (grads_out[k, rows, :].astype(F32) + grads_half[way].astype(F32)).astype(BF16)
        grad_copy(k).start()
    send_back(last_set, 3)
    for s in range(last_set):
        for n in range(1, SET):
            send_back(s, n)
    for step in range(1, half):
        parts = []
        for way in range(2):
            i = 2 * (half - step) - 1 + way
            ready(i)
            parts.append(combine(i))
        for way, part in ring_pieces(step):
            lanes = slice(part * latent, (part + 1) * latent)
            value = parts[way][part]
            if (way, part) in ring_pieces(step - 1):
                ring_copy(way, step - 1, part).wait_recv()
                value = value + ring_in[way, step - 1, :, lanes].astype(F32)
            ring_out[way, step, :, lanes] = value.astype(BF16)
            ring_copy(way, step, part).start()
    ready(0)
    parts = combine(0)
    for part in range(2):
        lanes = slice(part * latent, (part + 1) * latent)
        value = parts[part]
        for way in range(2):
            if (way, part) in ring_pieces(half - 1):
                ring_copy(way, half - 1, part).wait_recv()
                value = value + ring_in[way, half - 1, :, lanes].astype(F32)
        mid[:, lanes] = value.astype(BF16)

    block = latent // groups
    features = tokens_ref.shape[1]
    column_rows = features // columns
    ring_rows = column_rows // ring
    last_rows = ring_rows // CORES

    def late_lanes(k, c):
        start = latent * (1 - c) + block * lax.rem(my_group + k, groups)
        return pl.ds(pl.multiple_of(start, block), block)

    def late_copy(k, c):
        return pltpu.make_async_remote_copy(
            src_ref=mid.at[:, late_lanes(k, c)],
            dst_ref=lates.at[k, core],
            send_sem=late_send.at[k, c],
            recv_sem=late_recv.at[k, core],
            device_id=mate(k, c),
            device_id_type=MESH,
        )

    def late_arrived(k, c):
        pltpu.make_async_remote_copy(
            src_ref=lates.at[k, c],
            dst_ref=lates.at[k, c],
            send_sem=late_send.at[k, c],
            recv_sem=late_recv.at[k, c],
            device_id=mate(k, c),
            device_id_type=MESH,
        ).wait_recv()

    for k, c in mates:
        late_copy(k, c).start()
    lates[0, core] = mid[:, late_lanes(0, core)]
    mixed_ref[...] = dot(mid[:, 0:latent], up_ref[...], COLS)
    token_grad_ref[...] = dot(mid[:, latent:], down_ref[...], COLS)
    stores[0].start()
    stores[1].start()

    side_arrived(0, 1 - core)
    if across > 1:
        for c in range(CORES):
            side_arrived(across, c)
    for k, c in mates:
        late_arrived(k, c)
    both = groups * CORES * tokens_here
    late_columns = lates[...].reshape(both, block).astype(F32).T.astype(BF16)

    def term_rows(k):
        cols = pl.ds(pl.multiple_of(lax.rem(lax.div(me, ring * CORES) + k, columns) * column_rows, column_rows), column_rows)
        return dot(late_columns, sides[:, :, :, cols].reshape(both, column_rows)).T

    def x_copy(k):
        return pltpu.make_async_remote_copy(
            src_ref=x_out.at[k],
            dst_ref=x_in.at[k],
            send_sem=x_send.at[k],
            recv_sem=x_recv.at[k],
            device_id=at_peer(peer(k * CORES)),
            device_id_type=MESH,
        )

    for k in sorted(range(1, columns), key=lambda k: -min(k, columns - k)):
        x_out[k] = term_rows(k).astype(BF16)
        x_copy(k).start()
    total = term_rows(0)
    for k in near:
        grad_copy(k).wait_recv()
        gate_grad_ref[...] += grads_in[k, 0:latent, 0:share].astype(F32)
        up_grad_ref[...] += grads_in[k, 0:latent, share:].astype(F32)
        out_grad_ref[...] += grads_in[k, latent:, :].astype(F32)
    for store in stores[2:]:
        store.start()
    for k in range(1, columns):
        x_copy(k).wait_recv()
        total = total + x_in[k].astype(F32)
    x_sum[...] = total.reshape(ring, ring_rows, block)
    z_out[...] = x_sum[...].astype(BF16)

    def z_copy(r):
        return pltpu.make_async_remote_copy(
            src_ref=z_out.at[lax.rem(z + r, ring)],
            dst_ref=z_in.at[r],
            send_sem=z_send.at[r],
            recv_sem=z_recv.at[r],
            device_id=on_ring(r),
            device_id_type=MESH,
        )

    for r in range(1, ring):
        z_copy(r).start()
    total = x_sum[z]
    for r in range(1, ring):
        z_copy(r).wait_recv()
        total = total + z_in[r].astype(F32)
    last_out[...] = total.reshape(CORES, last_rows, block)

    def group_lanes(k):
        return pl.ds(pl.multiple_of(lax.rem(my_group + groups - k, groups) * block, block), block)

    def last_copy(k, c):
        return pltpu.make_async_remote_copy(
            src_ref=last_out.at[c],
            dst_ref=proj_hbm.at[core, :, group_lanes(0)],
            send_sem=last_send.at[k, c],
            recv_sem=last_recv.at[k, core],
            device_id=mate(k, c),
            device_id_type=MESH,
        )

    def last_arrived(k, c):
        pltpu.make_async_remote_copy(
            src_ref=last_out.at[c],
            dst_ref=proj_hbm.at[c, :, group_lanes(k)],
            send_sem=last_send.at[k, c],
            recv_sem=last_recv.at[k, c],
            device_id=mate(k, c),
            device_id_type=MESH,
        ).wait_recv()

    own_last = pltpu.make_async_copy(
        last_out.at[core], proj_hbm.at[core, :, group_lanes(0)], last_recv.at[0, core]
    )

    for k, c in mates:
        last_copy(k, c).start()
    own_last.start()

    own_last.wait()
    for k, c in mates:
        last_arrived(k, c)

    for k in near:
        for c in range(CORES):
            side_copy(k, c, tokens_ref).wait_send()
    side_copy(0, 1 - core, tokens_ref).wait_send()
    if across > 1:
        for c in range(CORES):
            relay_copy(c).wait_send()
    for k, c in mates:
        late_copy(k, c).wait_send()
        last_copy(k, c).wait_send()
    for k in range(1, columns):
        x_copy(k).wait_send()
    for r in range(1, ring):
        z_copy(r).wait_send()

    for step in range(half):
        for way, part in gather_pieces(step):
            gather_copy(way, step, part).wait_send()
        for way, part in ring_pieces(step):
            ring_copy(way, step, part).wait_send()

    def sent(j, carry):
        for chunk in range(len(chunks)):
            slot_copy(j, chunk, *chunks[chunk], all_lanes).wait_send()
        for s in range(sets):
            for n in range(SET):
                back_copy(j, s, n).wait_send()
        return carry

    lax.fori_loop(1, peers, sent, 0)
    for k in near:
        grad_copy(k).wait_send()
    if across > 1:
        for way in range(2):
            pass_copy(way).wait_send()
    for store in stores:
        store.wait()


def layer(ring, routes, gates, tokens, cotan, down, up, gate_weight, up_weight, out_weight):
    count, latent = tokens.shape[0], down.shape[1]
    hidden = gate_weight.shape[1]
    experts = lax.axis_size("expert")
    groups = lax.axis_size("dp")
    peers = experts // ring
    sets = ring // SET
    half = ring // 2
    share = hidden // groups
    chosen = 2 * peers * MAIN
    rows = sets * SET_ROWS
    features = tokens.shape[1]
    columns = peers // CORES
    block = latent // groups
    last_rows = features // experts
    ring_rows = last_rows * CORES
    vmem = pl.BlockSpec(memory_space=pltpu.VMEM)
    anywhere = pl.BlockSpec(memory_space=pl.ANY)
    dma = pltpu.SemaphoreType.DMA
    arrays = (tokens, cotan, down, up, gate_weight, up_weight, out_weight)
    results = (
        jax.ShapeDtypeStruct((count, features), F32),
        jax.ShapeDtypeStruct((count, features), F32),
        jax.ShapeDtypeStruct((CORES, last_rows, latent), F32),
        jax.ShapeDtypeStruct((latent, share), F32),
        jax.ShapeDtypeStruct((latent, share), F32),
        jax.ShapeDtypeStruct((share, latent), F32),
    )
    return pl.pallas_call(
        partial(layer_kernel, ring),
        out_shape=results,
        in_specs=[vmem] * 2 + [anywhere] * 7,
        out_specs=(anywhere,) * len(results),
        scratch_shapes=[pltpu.VMEM(a.shape, a.dtype) for a in arrays + results[:2] + results[3:]]
        + [
            dma((len(arrays),)),
            dma((len(results) - 1,)),
            pltpu.VMEM((count, 2 * latent), BF16),
            pltpu.VMEM((groups, CORES, count, features), BF16),
            pltpu.VMEM((groups, CORES, count, block), BF16),
            pltpu.VMEM((columns, features // columns, block), BF16),
            pltpu.VMEM((columns, features // columns, block), BF16),
            pltpu.VMEM((ring, ring_rows, block), F32),
            pltpu.VMEM((ring, ring_rows, block), BF16),
            pltpu.VMEM((ring, ring_rows, block), BF16),
            pltpu.VMEM((CORES, last_rows, block), F32),
            pltpu.VMEM((ring, count + MAIN, 2 * latent), BF16),
            pltpu.VMEM((peers, rows, 2 * latent), BF16),
            pltpu.VMEM((peers, rows, 2 * latent), BF16),
            pltpu.VMEM((peers, rows, 2 * latent), BF16),
            pltpu.VMEM((peers, rows, 2 * latent), BF16),
            pltpu.VMEM((ring, chosen, count), BF16),
            pltpu.VMEM((ring, chosen, count), BF16),
            pltpu.VMEM((peers * MAIN, 2 * latent), F32),
            pltpu.VMEM((peers, rows, hidden), BF16),
            pltpu.VMEM((peers, rows, hidden), BF16),
            pltpu.VMEM((peers, rows, hidden), BF16),
            pltpu.VMEM((2, half, count, 2 * latent), BF16),
            pltpu.VMEM((2, half, count, 2 * latent), BF16),
            pltpu.VMEM((groups, latent + share, 2 * share), BF16),
            pltpu.VMEM((groups, latent + share, 2 * share), BF16),
            pltpu.VMEM((2, (latent + share) // 2, 2 * share), BF16),
            dma((2, half, 2)),
            dma((2, half, 2)),
            dma((sets + 1, peers)),
            dma((sets + 1, peers)),
            dma((sets, SET, peers)),
            dma((sets, SET, peers)),
            dma((1 + SET, sets + 1)),
            dma((2, half, 2)),
            dma((2, half, 2)),
            dma((groups,)),
            dma((groups,)),
            dma((2,)),
            dma((2,)),
            dma((groups, CORES)),
            dma((groups, CORES)),
            dma((CORES,)),
            dma((groups, CORES)),
            dma((groups, CORES)),
            dma((columns,)),
            dma((columns,)),
            dma((ring,)),
            dma((ring,)),
            dma((groups, CORES)),
            dma((groups, CORES)),
        ],
        compiler_params=pltpu.CompilerParams(
            collective_id=0, has_side_effects=True, vmem_limit_bytes=60 * 1024 * 1024
        ),
        name="layer",
    )(routes, gates, tokens, cotan, down, up, gate_weight, up_weight, out_weight)


def shards(
    ring,
    tokens,
    routes,
    gate_values,
    latent_down,
    gate_weight,
    up_weight,
    out_weight,
    latent_up,
    grad_mixed,
):
    mixed, grad_tokens, proj_grads, gate_grad, up_grad, out_grad = layer(
        ring,
        routes.T,
        gate_values.T,
        tokens,
        grad_mixed,
        latent_down,
        latent_up,
        gate_weight[0],
        up_weight[0],
        out_weight[0],
    )
    mixed, grad_tokens = mixed.astype(BF16), grad_tokens.astype(BF16)
    return mixed, grad_tokens, proj_grads[0], proj_grads[1], gate_grad[None], up_grad[None], out_grad[None]


def solution(mesh, ring=RING):
    rows = P(("dp", "expert"), None)
    own = P("expert", None, None)
    return jax.shard_map(
        partial(shards, ring),
        mesh=mesh,
        in_specs=(rows, rows, rows, P(), own, own, own, P(), rows),
        out_specs=(
            rows,
            rows,
            P("expert", None),
            P("expert", None),
            P("expert", None, "dp"),
            P("expert", None, "dp"),
            P("expert", "dp", None),
        ),
        check_vma=False,
    )
```

```python
from functools import partial

import jax
import jax.numpy as jnp
from jax import lax
from jax.experimental import pallas as pl
from jax.experimental.pallas import tpu as pltpu
from jax.sharding import PartitionSpec as P

MESH = pl.DeviceIdType.MESH
ROWS = (((0,), (0,)), ((), ()))
COLS = (((1,), (1,)), ((), ()))
PLAIN = (((1,), (0,)), ((), ()))
F32 = jnp.float32
BF16 = jnp.bfloat16

RING = 8
CORES = 2
CAP = 20
MAIN = 16
EXTRA = 4
SET = 4
SET_ROWS = SET * CAP


def dot(a, b, dims=PLAIN):
    return lax.dot_general(a, b, dims, preferred_element_type=F32)


def layer_kernel(
    ring,
    routes_ref,
    gates_ref,
    tokens_hbm,
    cotan_hbm,
    down_hbm,
    up_hbm,
    gw_hbm,
    uw_hbm,
    ow_hbm,
    mixed_hbm,
    token_grad_hbm,
    proj_hbm,
    gate_grad_hbm,
    up_grad_hbm,
    out_grad_hbm,
    tokens_ref,
    cotan_ref,
    down_ref,
    up_ref,
    gw_ref,
    uw_ref,
    ow_ref,
    mixed_ref,
    token_grad_ref,
    gate_grad_ref,
    up_grad_ref,
    out_grad_ref,
    load_sem,
    store_sem,
    mid,
    sides,
    lates,
    term_sum,
    x_out,
    x_in,
    x_sum,
    z_out,
    z_in,
    last_out,
    gathered,
    send_rows,
    expert_rows,
    result_rows,
    back_rows,
    pick,
    weigh,
    extra_sum,
    act,
    grad_gate,
    grad_up,
    ring_out,
    ring_in,
    grads_out,
    grads_in,
    grads_half,
    gather_send,
    gather_recv,
    slot_send,
    slot_recv,
    back_send,
    back_recv,
    own_sem,
    ring_send,
    ring_recv,
    grad_send,
    grad_recv,
    half_send,
    half_recv,
    side_send,
    side_recv,
    relay_send,
    late_send,
    late_recv,
    x_send,
    x_recv,
    z_send,
    z_recv,
    last_send,
    last_recv,
):
    tokens_here, latent = tokens_ref.shape[0], down_ref.shape[1]
    hidden = gw_ref.shape[1]
    experts = lax.axis_size("expert")
    groups = lax.axis_size("dp")
    columns = experts // (ring * CORES)
    peers = columns * CORES
    half = ring // 2
    sets = ring // SET
    me = lax.axis_index("expert")
    my_group = lax.axis_index("dp")
    z = lax.rem(lax.div(me, CORES), ring)
    core = lax.rem(me, CORES)
    place = lax.div(me, ring * CORES) * CORES + core

    def on_ring(step):
        other = lax.rem(z + step + ring, ring)
        return (my_group, me + (other - z) * CORES)

    def at_peer(d):
        return (my_group, (lax.div(d, CORES) * ring + z) * CORES + lax.rem(d, CORES))

    def peer(j):
        return lax.rem(place + j, peers)

    def group_at(k):
        return (lax.rem(my_group + k, groups), me)

    def mate(k, c):
        return (lax.rem(my_group + k, groups), me - core + c)

    mates = [(k, c) for k in range(1, groups) for c in range(CORES)] + [(0, 1 - core)]

    barrier = pltpu.get_barrier_semaphore()
    for step in range(1, ring):
        pl.semaphore_signal(barrier, inc=1, device_id=on_ring(step), device_id_type=MESH)
    for j in range(1, peers):
        pl.semaphore_signal(barrier, inc=1, device_id=at_peer(peer(j)), device_id_type=MESH)
    for k, c in mates:
        pl.semaphore_signal(barrier, inc=1, device_id=mate(k, c), device_id_type=MESH)

    loads = [
        pltpu.make_async_copy(src, dst, load_sem.at[n])
        for n, (src, dst) in enumerate(
            (
                (tokens_hbm, tokens_ref),
                (down_hbm, down_ref),
                (cotan_hbm, cotan_ref),
                (up_hbm, up_ref),
                (gw_hbm, gw_ref),
                (uw_hbm, uw_ref),
                (ow_hbm, ow_ref),
            )
        )
    ]
    stores = [
        pltpu.make_async_copy(src, dst, store_sem.at[n])
        for n, (src, dst) in enumerate(
            (
                (mixed_ref, mixed_hbm),
                (token_grad_ref, token_grad_hbm),
                (gate_grad_ref, gate_grad_hbm),
                (up_grad_ref, up_grad_hbm),
                (out_grad_ref, out_grad_hbm),
            )
        )
    ]
    for load in loads[:2]:
        load.start()

    expert_ids = lax.broadcasted_iota(jnp.int32, (experts, tokens_here), 0)
    table = jnp.zeros((experts, tokens_here), F32)
    for k in range(routes_ref.shape[0]):
        table = table + jnp.where(expert_ids == routes_ref[k : k + 1, :], gates_ref[k : k + 1, :], 0.0)
    table = table.astype(BF16)
    per_column = ring * CORES
    for b in range(columns):
        rows = slice(b * per_column, (b + 1) * per_column)
        lanes = slice(b * tokens_here, (b + 1) * tokens_here)
        gathered[0, tokens_here : tokens_here + per_column, lanes] = table[rows, :]

    def gather_copy(way, step, part):
        source = 0 if step == 0 else 2 * step - 1 + way
        target = 2 * step + 1 + way if step < half - 1 else ring - 1
        rows = pl.ds(0, tokens_here + MAIN if part == 0 else tokens_here)
        lanes = pl.ds(part * latent, latent)
        return pltpu.make_async_remote_copy(
            src_ref=gathered.at[source, rows, lanes],
            dst_ref=gathered.at[target, rows, lanes],
            send_sem=gather_send.at[way, step, part],
            recv_sem=gather_recv.at[way, step, part],
            device_id=on_ring(1 if way == 0 else -1),
            device_id_type=MESH,
        )

    def gather_pieces(step):
        return [(way, part) for part in range(2) for way in range(2) if step < half - 1 or part == way]

    loads[0].wait()
    loads[1].wait()
    for load in loads[2:4]:
        load.start()
    gathered[0, 0:tokens_here, 0:latent] = dot(tokens_ref[...], down_ref[...]).astype(BF16)
    pl.semaphore_wait(barrier, (ring - 1) + (peers - 1) + len(mates))
    for way in range(2):
        gather_copy(way, 0, 0).start()
    loads[2].wait()
    loads[3].wait()
    gathered[0, 0:tokens_here, latent:] = dot(cotan_ref[...], up_ref[...]).astype(BF16)
    for way in range(2):
        gather_copy(way, 0, 1).start()
    for load in loads[4:]:
        load.start()

    earlier = (
        lax.broadcasted_iota(jnp.int32, (tokens_here, tokens_here), 0)
        < lax.broadcasted_iota(jnp.int32, (tokens_here, tokens_here), 1)
    ).astype(BF16)
    row_ids = lax.broadcasted_iota(jnp.int32, (per_column, tokens_here), 0)
    main_slots = lax.broadcasted_iota(jnp.int32, (MAIN, tokens_here), 0).astype(F32)

    last_set = sets - 1
    near_rows = (SET - 1) * MAIN
    chunks = [(s * SET_ROWS, SET_ROWS) for s in range(last_set)] + [
        (last_set * SET_ROWS, near_rows),
        (last_set * SET_ROWS + near_rows, SET_ROWS - near_rows),
    ]

    def chunk_of(i):
        return i // SET + (1 if i == ring - 1 else 0)

    def slot_copy(j, chunk, first, count, lanes):
        d = peer(j)
        rows = pl.ds(first, count)
        return pltpu.make_async_remote_copy(
            src_ref=send_rows.at[d, rows, lanes],
            dst_ref=expert_rows.at[place, rows, lanes],
            send_sem=slot_send.at[chunk, j],
            recv_sem=slot_recv.at[chunk, j],
            device_id=at_peer(d),
            device_id_type=MESH,
        )

    def own_slots(chunk, first, count, lanes):
        rows = pl.ds(first, count)
        return pltpu.make_async_copy(
            send_rows.at[place, rows, lanes], expert_rows.at[place, rows, lanes], own_sem.at[0, chunk]
        )

    all_lanes = pl.ds(0, 2 * latent)

    def table_rows(i):
        found = []
        for b in range(columns):
            first = b * tokens_here
            info = gathered[i, tokens_here : tokens_here + per_column, first : first + tokens_here].astype(F32)
            for c in range(CORES):
                found.append(jnp.sum(jnp.where(row_ids == z * CORES + c, info, 0.0), axis=0, keepdims=True))
        return jnp.concatenate(found, axis=0)

    main_count = peers * MAIN

    def dispatch(i, part):
        s, within = i // SET, i % SET
        lanes = slice(part * latent, (part + 1) * latent)
        if part == 0:
            named = table_rows(i) > 0.0
            before = dot(named.astype(F32).astype(BF16), earlier)
            slot = jnp.where(named, before, -1.0)
            extra_rows = lax.broadcasted_iota(jnp.int32, (MAIN, tokens_here), 0)
            extra_slots = jnp.where(
                lax.div(extra_rows, EXTRA) == within, MAIN + lax.rem(extra_rows, EXTRA), -2
            ).astype(F32)
            hits = []
            for slots in (main_slots, extra_slots):
                for d in range(peers):
                    hits.append((slots == slot[d : d + 1, :]).astype(F32))
            chosen = jnp.concatenate(hits, axis=0).astype(BF16)
            pick[i] = chosen
            rows = dot(chosen, gathered[i, 0:tokens_here, lanes])
        else:
            weight = table_rows(i)
            weight_rows = jnp.concatenate(
                [jnp.broadcast_to(weight[d : d + 1, :], (MAIN, tokens_here)) for d in range(peers)], axis=0
            )
            chosen = pick[i]
            weighted = chosen.astype(F32) * jnp.concatenate([weight_rows, weight_rows], axis=0)
            weigh[i] = weighted.astype(BF16)
            scale = jnp.sum(weighted, axis=1, keepdims=True)
            rows = dot(chosen, gathered[i, 0:tokens_here, lanes]) * scale
        first = s * SET_ROWS + within * MAIN
        send_rows[:, first : first + MAIN, lanes] = rows[:main_count].astype(BF16).reshape(peers, MAIN, latent)
        extra = rows[main_count:]
        if within > 0:
            extra = extra + extra_sum[:, lanes]
        if within < SET - 1:
            extra_sum[:, lanes] = extra
        else:
            first = s * SET_ROWS + SET * MAIN
            send_rows[:, first : first + MAIN, lanes] = extra.astype(BF16).reshape(peers, MAIN, latent)
        count = MAIN if within < SET - 1 else 2 * MAIN
        lanes = pl.ds(part * latent, latent)

        def start(j, carry):
            slot_copy(j, chunk_of(i), s * SET_ROWS + within * MAIN, count, lanes).start()
            return carry

        lax.fori_loop(1, peers, start, 0)
        own_slots(chunk_of(i), s * SET_ROWS + within * MAIN, count, lanes).start()

    def side_copy(k, c, source):
        return pltpu.make_async_remote_copy(
            src_ref=source,
            dst_ref=sides.at[k, core],
            send_sem=side_send.at[k, c],
            recv_sem=side_recv.at[k, core],
            device_id=mate(k, c),
            device_id_type=MESH,
        )

    def side_arrived(k, c):
        pltpu.make_async_remote_copy(
            src_ref=tokens_ref,
            dst_ref=sides.at[k, c],
            send_sem=side_send.at[k, c],
            recv_sem=side_recv.at[k, c],
            device_id=mate(k, c),
            device_id_type=MESH,
        ).wait_recv()

    across = groups // 2

    def relay_copy(c):
        step = 1 - 2 * core
        return pltpu.make_async_remote_copy(
            src_ref=sides.at[1 + (groups - 2) * core, c],
            dst_ref=sides.at[across, c],
            send_sem=relay_send.at[c],
            recv_sem=side_recv.at[across, c],
            device_id=(lax.rem(my_group + step + groups, groups), me),
            device_id_type=MESH,
        )

    for part in range(2):
        dispatch(0, part)
    near = sorted({1, groups - 1})
    for k in near:
        for c, source in enumerate((tokens_ref, cotan_ref)):
            side_copy(k, c, source).start()

    @pl.when(core == 0)
    def _():
        side_copy(0, 1, cotan_ref).start()

    @pl.when(core == 1)
    def _():
        side_copy(0, 0, tokens_ref).start()

    sides[0, core] = jnp.where(core == 0, tokens_ref[...], cotan_ref[...])
    for step in range(1, half):
        for part in range(2):
            for way in range(2):
                gather_copy(way, step - 1, part).wait_recv()
                if (way, part) in gather_pieces(step):
                    gather_copy(way, step, part).start()
            for way in range(2):
                dispatch(2 * step - 1 + way, part)

    back_pieces = [((SET - 1) * MAIN, 2 * MAIN)] + [(n * MAIN, MAIN) for n in range(SET - 2, -1, -1)]

    def back_copy(j, s, n):
        d = peer(j)
        first, count = back_pieces[n]
        rows = pl.ds(s * SET_ROWS + first, count)
        return pltpu.make_async_remote_copy(
            src_ref=result_rows.at[d, rows],
            dst_ref=back_rows.at[place, rows],
            send_sem=back_send.at[s, n, j],
            recv_sem=back_recv.at[s, n, j],
            device_id=at_peer(d),
            device_id_type=MESH,
        )

    def own_back(s, n):
        first, count = back_pieces[n]
        rows = pl.ds(s * SET_ROWS + first, count)
        return pltpu.make_async_copy(result_rows.at[place, rows], back_rows.at[place, rows], own_sem.at[1 + n, s])

    tile = min(256, hidden)
    wide = min(256, latent)
    def send_back(s, n):
        def start(j, carry):
            back_copy(j, s, n).start()
            return carry

        lax.fori_loop(1, peers, start, 0)
        own_back(s, n).start()

    def slots_arrived(chunk):
        def arrived(j, carry):
            slot_copy(j, chunk, *chunks[chunk], all_lanes).wait_recv()
            return carry

        lax.fori_loop(1, peers, arrived, 0)
        own_slots(chunk, *chunks[chunk], all_lanes).wait()

    def expert(chunk):
        first, per_peer = chunks[chunk]
        set_rows = slice(first, first + per_peer)
        count = peers * per_peer

        def hidden_tile(h, carry):
            cols = pl.ds(pl.multiple_of(h * tile, tile), tile)
            rows_in = expert_rows[:, set_rows, 0:latent].reshape(count, latent)
            grad_in = expert_rows[:, set_rows, latent:].reshape(count, latent)
            pre_gate = dot(rows_in, gw_ref[:, cols])
            pre_up = dot(rows_in, uw_ref[:, cols])
            grad_act = dot(grad_in, ow_ref[cols, :], COLS)
            sig = 1.0 / (1.0 + jnp.exp(-pre_gate))
            swish = pre_gate * sig
            shape = (peers, per_peer, tile)
            act[:, set_rows, cols] = (swish * pre_up).astype(BF16).reshape(shape)
            grad_gate[:, set_rows, cols] = (
                (grad_act * pre_up * (sig * (1.0 + pre_gate * (1.0 - sig)))).astype(BF16).reshape(shape)
            )
            grad_up[:, set_rows, cols] = (grad_act * swish).astype(BF16).reshape(shape)
            return carry

        lax.fori_loop(0, hidden // tile, hidden_tile, 0)

        def latent_tile(n, carry):
            cols = pl.ds(pl.multiple_of(n * wide, wide), wide)
            later = pl.ds(pl.multiple_of(latent + n * wide, wide), wide)
            shape = (peers, per_peer, wide)
            out = dot(act[:, set_rows, :].reshape(count, hidden), ow_ref[:, cols])
            result_rows[:, set_rows, cols] = out.astype(BF16).reshape(shape)
            back = dot(grad_gate[:, set_rows, :].reshape(count, hidden), gw_ref[cols, :], COLS)
            back = back + dot(grad_up[:, set_rows, :].reshape(count, hidden), uw_ref[cols, :], COLS)
            result_rows[:, set_rows, later] = back.astype(BF16).reshape(shape)
            return carry

        lax.fori_loop(0, latent // wide, latent_tile, 0)


    for load in loads[4:]:
        load.wait()
    for chunk in range(last_set):
        slots_arrived(chunk)
        expert(chunk)
    for way, part in gather_pieces(half - 1):
        gather_copy(way, half - 1, part).wait_recv()
    for part in range(2):
        dispatch(ring - 1, part)
    slots_arrived(last_set)
    expert(last_set)
    for c in range(CORES):
        for k in near:
            side_arrived(k, c)
    if across > 1:
        for c in range(CORES):
            relay_copy(c).start()
    slots_arrived(last_set + 1)
    for s in range(last_set):
        send_back(s, 0)
    expert(last_set + 1)
    send_back(last_set, 0)
    send_back(last_set, 1)
    send_back(last_set, 2)
    send_back(last_set, 3)
    for s in range(last_set):
        for n in range(1, SET):
            send_back(s, n)

    share = hidden // groups
    all_rows = peers * sets * SET_ROWS

    def grad_copy(k):
        return pltpu.make_async_remote_copy(
            src_ref=grads_out.at[k],
            dst_ref=grads_in.at[k],
            send_sem=grad_send.at[k],
            recv_sem=grad_recv.at[k],
            device_id=group_at(k),
            device_id_type=MESH,
        )

    def weight_terms(k):
        cols = pl.ds(pl.multiple_of(lax.rem(my_group + k, groups) * share, share), share)
        rows_in = expert_rows[:, :, 0:latent].reshape(all_rows, latent)
        grad_in = expert_rows[:, :, latent:].reshape(all_rows, latent)
        gate_term = dot(rows_in, grad_gate[:, :, cols].reshape(all_rows, share), ROWS)
        up_term = dot(rows_in, grad_up[:, :, cols].reshape(all_rows, share), ROWS)
        out_term = dot(act[:, :, cols].reshape(all_rows, share), grad_in, ROWS)
        return gate_term, up_term, out_term

    def other_share(k, carry):
        gate_term, up_term, out_term = weight_terms(k)
        grads_out[k, 0:latent, 0:share] = gate_term.astype(BF16)
        grads_out[k, 0:latent, share:] = up_term.astype(BF16)
        grads_out[k, latent:, :] = out_term.astype(BF16)
        return carry

    half_rows = (latent + share) // 2

    def pass_copy(way):
        return pltpu.make_async_remote_copy(
            src_ref=grads_out.at[across, pl.ds(way * half_rows, half_rows)],
            dst_ref=grads_half.at[way],
            send_sem=half_send.at[way],
            recv_sem=half_recv.at[way],
            device_id=group_at(near[way]),
            device_id_type=MESH,
        )

    if across > 1:
        lax.fori_loop(across, across + 1, other_share, 0)
        for way in range(2):
            pass_copy(way).start()
    lax.fori_loop(0, len(near), lambda n, carry: other_share(1 + (groups - 2) * n, carry), 0)

    def combine(i):
        s, within = i // SET, i % SET
        first = s * SET_ROWS + within * MAIN
        extra = s * SET_ROWS + SET * MAIN
        shape = (peers * MAIN, latent)
        parts = []
        for part, matrix in enumerate((weigh, pick)):
            lanes = slice(part * latent, (part + 1) * latent)
            rows = jnp.concatenate(
                [
                    back_rows[:, first : first + MAIN, lanes].reshape(shape),
                    back_rows[:, extra : extra + MAIN, lanes].reshape(shape),
                ],
                axis=0,
            )
            parts.append(dot(matrix[i], rows, ROWS))
        return parts

    def ring_copy(way, step, part):
        lanes = pl.ds(part * latent, latent)
        return pltpu.make_async_remote_copy(
            src_ref=ring_out.at[way, step, :, lanes],
            dst_ref=ring_in.at[way, step, :, lanes],
            send_sem=ring_send.at[way, step, part],
            recv_sem=ring_recv.at[way, step, part],
            device_id=on_ring(-1 if way == 0 else 1),
            device_id_type=MESH,
        )

    def ring_pieces(step):
        pieces = [(way, 1 - way) for way in range(2)] if step > 0 else []
        return pieces + [(way, way) for way in range(2)]

    arrived_pieces = set()

    def ready(i):
        s = i // SET
        n = SET - 1 - i % SET
        if (s, n) in arrived_pieces:
            return
        arrived_pieces.add((s, n))

        def arrived(j, carry):
            back_copy(j, s, n).wait_recv()
            return carry

        lax.fori_loop(1, peers, arrived, 0)
        own_back(s, n).wait()

    ready(ring - 1)
    parts = combine(ring - 1)
    for way, part in ring_pieces(0):
        ring_out[way, 0, :, part * latent : (part + 1) * latent] = parts[part].astype(BF16)
        ring_copy(way, 0, part).start()
    gate_grad_ref[...], up_grad_ref[...], out_grad_ref[...] = weight_terms(0)
    for way, k in enumerate(near):
        if across > 1:
            pass_copy(way).wait_recv()
            rows = slice(way * half_rows, (way + 1) * half_rows)
            grads_out[k, rows, :] = (grads_out[k, rows, :].astype(F32) + grads_half[way].astype(F32)).astype(BF16)
        grad_copy(k).start()
    for step in range(1, half):
        parts = []
        for way in range(2):
            i = 2 * (half - step) - 1 + way
            ready(i)
            parts.append(combine(i))
        for way, part in ring_pieces(step):
            lanes = slice(part * latent, (part + 1) * latent)
            value = parts[way][part]
            if (way, part) in ring_pieces(step - 1):
                ring_copy(way, step - 1, part).wait_recv()
                value = value + ring_in[way, step - 1, :, lanes].astype(F32)
            ring_out[way, step, :, lanes] = value.astype(BF16)
            ring_copy(way, step, part).start()
    block = latent // groups
    features = tokens_ref.shape[1]
    column_rows = features // columns
    ring_rows = column_rows // ring
    last_rows = ring_rows // CORES

    def late_lanes(k, c):
        start = latent * (1 - c) + block * lax.rem(my_group + k, groups)
        return pl.ds(pl.multiple_of(start, block), block)

    def late_copy(k, c):
        return pltpu.make_async_remote_copy(
            src_ref=mid.at[:, late_lanes(k, c)],
            dst_ref=lates.at[k, core],
            send_sem=late_send.at[k, c],
            recv_sem=late_recv.at[k, core],
            device_id=mate(k, c),
            device_id_type=MESH,
        )

    def late_arrived(k, c):
        pltpu.make_async_remote_copy(
            src_ref=lates.at[k, c],
            dst_ref=lates.at[k, c],
            send_sem=late_send.at[k, c],
            recv_sem=late_recv.at[k, c],
            device_id=mate(k, c),
            device_id_type=MESH,
        ).wait_recv()

    ready(0)
    parts = combine(0)
    for part in range(2):
        lanes = slice(part * latent, (part + 1) * latent)
        value = parts[part]
        for way in range(2):
            if (way, part) in ring_pieces(half - 1):
                ring_copy(way, half - 1, part).wait_recv()
                value = value + ring_in[way, half - 1, :, lanes].astype(F32)
        mid[:, lanes] = value.astype(BF16)
        for k in range(1, groups):
            late_copy(k, 1 - part).start()
    late_copy(0, 1 - core).start()
    lates[0, core] = mid[:, late_lanes(0, core)]

    pair = CORES * tokens_here

    def late_columns(k):
        return lates[k].reshape(pair, block).astype(F32).T.astype(BF16)

    side_arrived(0, 1 - core)
    late_arrived(0, 1 - core)
    term_sum[...] = dot(late_columns(0), sides[0].reshape(pair, features))
    for k in near:
        if k != across:
            for c in range(CORES):
                late_arrived(k, c)
            term_sum[...] += dot(late_columns(k), sides[k].reshape(pair, features))
    for c in range(CORES):
        if across > 1:
            side_arrived(across, c)
        late_arrived(across, c)
    last_columns = late_columns(across)

    def term_rows(k):
        first = lax.rem(lax.div(me, ring * CORES) + k, columns) * column_rows
        cols = pl.ds(pl.multiple_of(first, column_rows), column_rows)
        term = dot(last_columns, sides[across, :, :, cols].reshape(pair, column_rows))
        return (term_sum[:, cols] + term).T

    def x_copy(k):
        return pltpu.make_async_remote_copy(
            src_ref=x_out.at[k],
            dst_ref=x_in.at[k],
            send_sem=x_send.at[k],
            recv_sem=x_recv.at[k],
            device_id=at_peer(peer(k * CORES)),
            device_id_type=MESH,
        )

    for k in sorted(range(1, columns), key=lambda k: -min(k, columns - k)):
        x_out[k] = term_rows(k).astype(BF16)
        x_copy(k).start()
    total = term_rows(0)
    mixed_ref[...] = dot(mid[:, 0:latent], up_ref[...], COLS)
    stores[0].start()
    token_grad_ref[...] = dot(mid[:, latent:], down_ref[...], COLS)
    stores[1].start()
    for k in near:
        grad_copy(k).wait_recv()
        gate_grad_ref[...] += grads_in[k, 0:latent, 0:share].astype(F32)
        up_grad_ref[...] += grads_in[k, 0:latent, share:].astype(F32)
        out_grad_ref[...] += grads_in[k, latent:, :].astype(F32)
    for store in stores[2:]:
        store.start()
    for k in range(1, columns):
        x_copy(k).wait_recv()
        total = total + x_in[k].astype(F32)
    x_sum[...] = total.reshape(ring, ring_rows, block)
    z_out[...] = x_sum[...].astype(BF16)

    def z_copy(r):
        return pltpu.make_async_remote_copy(
            src_ref=z_out.at[lax.rem(z + r, ring)],
            dst_ref=z_in.at[r],
            send_sem=z_send.at[r],
            recv_sem=z_recv.at[r],
            device_id=on_ring(r),
            device_id_type=MESH,
        )

    for r in range(1, ring):
        z_copy(r).start()
    total = x_sum[z]
    for r in range(1, ring):
        z_copy(r).wait_recv()
        total = total + z_in[r].astype(F32)
    last_out[...] = total.reshape(CORES, last_rows, block)

    def group_lanes(k):
        return pl.ds(pl.multiple_of(lax.rem(my_group + groups - k, groups) * block, block), block)

    def last_copy(k, c):
        return pltpu.make_async_remote_copy(
            src_ref=last_out.at[c],
            dst_ref=proj_hbm.at[core, :, group_lanes(0)],
            send_sem=last_send.at[k, c],
            recv_sem=last_recv.at[k, core],
            device_id=mate(k, c),
            device_id_type=MESH,
        )

    def last_arrived(k, c):
        pltpu.make_async_remote_copy(
            src_ref=last_out.at[c],
            dst_ref=proj_hbm.at[c, :, group_lanes(k)],
            send_sem=last_send.at[k, c],
            recv_sem=last_recv.at[k, c],
            device_id=mate(k, c),
            device_id_type=MESH,
        ).wait_recv()

    own_last = pltpu.make_async_copy(
        last_out.at[core], proj_hbm.at[core, :, group_lanes(0)], last_recv.at[0, core]
    )

    for k, c in mates:
        last_copy(k, c).start()
    own_last.start()

    own_last.wait()
    for k, c in mates:
        last_arrived(k, c)

    for k in near:
        for c in range(CORES):
            side_copy(k, c, tokens_ref).wait_send()
    side_copy(0, 1 - core, tokens_ref).wait_send()
    if across > 1:
        for c in range(CORES):
            relay_copy(c).wait_send()
    for k, c in mates:
        late_copy(k, c).wait_send()
        last_copy(k, c).wait_send()
    for k in range(1, columns):
        x_copy(k).wait_send()
    for r in range(1, ring):
        z_copy(r).wait_send()

    for step in range(half):
        for way, part in gather_pieces(step):
            gather_copy(way, step, part).wait_send()
        for way, part in ring_pieces(step):
            ring_copy(way, step, part).wait_send()

    def sent(j, carry):
        for chunk in range(len(chunks)):
            slot_copy(j, chunk, *chunks[chunk], all_lanes).wait_send()
        for s in range(sets):
            for n in range(SET):
                back_copy(j, s, n).wait_send()
        return carry

    lax.fori_loop(1, peers, sent, 0)
    for k in near:
        grad_copy(k).wait_send()
    if across > 1:
        for way in range(2):
            pass_copy(way).wait_send()
    for store in stores:
        store.wait()


def layer(ring, routes, gates, tokens, cotan, down, up, gate_weight, up_weight, out_weight):
    count, latent = tokens.shape[0], down.shape[1]
    hidden = gate_weight.shape[1]
    experts = lax.axis_size("expert")
    groups = lax.axis_size("dp")
    peers = experts // ring
    sets = ring // SET
    half = ring // 2
    share = hidden // groups
    chosen = 2 * peers * MAIN
    rows = sets * SET_ROWS
    features = tokens.shape[1]
    columns = peers // CORES
    block = latent // groups
    last_rows = features // experts
    ring_rows = last_rows * CORES
    vmem = pl.BlockSpec(memory_space=pltpu.VMEM)
    anywhere = pl.BlockSpec(memory_space=pl.ANY)
    dma = pltpu.SemaphoreType.DMA
    arrays = (tokens, cotan, down, up, gate_weight, up_weight, out_weight)
    results = (
        jax.ShapeDtypeStruct((count, features), F32),
        jax.ShapeDtypeStruct((count, features), F32),
        jax.ShapeDtypeStruct((CORES, last_rows, latent), F32),
        jax.ShapeDtypeStruct((latent, share), F32),
        jax.ShapeDtypeStruct((latent, share), F32),
        jax.ShapeDtypeStruct((share, latent), F32),
    )
    return pl.pallas_call(
        partial(layer_kernel, ring),
        out_shape=results,
        in_specs=[vmem] * 2 + [anywhere] * 7,
        out_specs=(anywhere,) * len(results),
        scratch_shapes=[pltpu.VMEM(a.shape, a.dtype) for a in arrays + results[:2] + results[3:]]
        + [
            dma((len(arrays),)),
            dma((len(results) - 1,)),
            pltpu.VMEM((count, 2 * latent), BF16),
            pltpu.VMEM((groups, CORES, count, features), BF16),
            pltpu.VMEM((groups, CORES, count, block), BF16),
            pltpu.VMEM((block, features), F32),
            pltpu.VMEM((columns, features // columns, block), BF16),
            pltpu.VMEM((columns, features // columns, block), BF16),
            pltpu.VMEM((ring, ring_rows, block), F32),
            pltpu.VMEM((ring, ring_rows, block), BF16),
            pltpu.VMEM((ring, ring_rows, block), BF16),
            pltpu.VMEM((CORES, last_rows, block), F32),
            pltpu.VMEM((ring, count + MAIN, 2 * latent), BF16),
            pltpu.VMEM((peers, rows, 2 * latent), BF16),
            pltpu.VMEM((peers, rows, 2 * latent), BF16),
            pltpu.VMEM((peers, rows, 2 * latent), BF16),
            pltpu.VMEM((peers, rows, 2 * latent), BF16),
            pltpu.VMEM((ring, chosen, count), BF16),
            pltpu.VMEM((ring, chosen, count), BF16),
            pltpu.VMEM((peers * MAIN, 2 * latent), F32),
            pltpu.VMEM((peers, rows, hidden), BF16),
            pltpu.VMEM((peers, rows, hidden), BF16),
            pltpu.VMEM((peers, rows, hidden), BF16),
            pltpu.VMEM((2, half, count, 2 * latent), BF16),
            pltpu.VMEM((2, half, count, 2 * latent), BF16),
            pltpu.VMEM((groups, latent + share, 2 * share), BF16),
            pltpu.VMEM((groups, latent + share, 2 * share), BF16),
            pltpu.VMEM((2, (latent + share) // 2, 2 * share), BF16),
            dma((2, half, 2)),
            dma((2, half, 2)),
            dma((sets + 1, peers)),
            dma((sets + 1, peers)),
            dma((sets, SET, peers)),
            dma((sets, SET, peers)),
            dma((1 + SET, sets + 1)),
            dma((2, half, 2)),
            dma((2, half, 2)),
            dma((groups,)),
            dma((groups,)),
            dma((2,)),
            dma((2,)),
            dma((groups, CORES)),
            dma((groups, CORES)),
            dma((CORES,)),
            dma((groups, CORES)),
            dma((groups, CORES)),
            dma((columns,)),
            dma((columns,)),
            dma((ring,)),
            dma((ring,)),
            dma((groups, CORES)),
            dma((groups, CORES)),
        ],
        compiler_params=pltpu.CompilerParams(
            collective_id=0, has_side_effects=True, vmem_limit_bytes=60 * 1024 * 1024
        ),
        name="layer",
    )(routes, gates, tokens, cotan, down, up, gate_weight, up_weight, out_weight)


def shards(
    ring,
    tokens,
    routes,
    gate_values,
    latent_down,
    gate_weight,
    up_weight,
    out_weight,
    latent_up,
    grad_mixed,
):
    mixed, grad_tokens, proj_grads, gate_grad, up_grad, out_grad = layer(
        ring,
        routes.T,
        gate_values.T,
        tokens,
        grad_mixed,
        latent_down,
        latent_up,
        gate_weight[0],
        up_weight[0],
        out_weight[0],
    )
    mixed, grad_tokens = mixed.astype(BF16), grad_tokens.astype(BF16)
    return mixed, grad_tokens, proj_grads[0], proj_grads[1], gate_grad[None], up_grad[None], out_grad[None]


def solution(mesh, ring=RING):
    rows = P(("dp", "expert"), None)
    own = P("expert", None, None)
    return jax.shard_map(
        partial(shards, ring),
        mesh=mesh,
        in_specs=(rows, rows, rows, P(), own, own, own, P(), rows),
        out_specs=(
            rows,
            rows,
            P("expert", None),
            P("expert", None),
            P("expert", None, "dp"),
            P("expert", None, "dp"),
            P("expert", "dp", None),
        ),
        check_vma=False,
    )
```

```python
from functools import partial

import jax
import jax.numpy as jnp
from jax import lax
from jax.experimental import pallas as pl
from jax.experimental.pallas import tpu as pltpu
from jax.sharding import PartitionSpec as P

MESH = pl.DeviceIdType.MESH
ROWS = (((0,), (0,)), ((), ()))
COLS = (((1,), (1,)), ((), ()))
PLAIN = (((1,), (0,)), ((), ()))
F32 = jnp.float32
BF16 = jnp.bfloat16

RING = 8
CORES = 2
CAP = 20
MAIN = 16
EXTRA = 4
SET = 4
SET_ROWS = SET * CAP


def dot(a, b, dims=PLAIN):
    return lax.dot_general(a, b, dims, preferred_element_type=F32)


def layer_kernel(
    ring,
    routes_ref,
    gates_ref,
    tokens_hbm,
    cotan_hbm,
    down_hbm,
    up_hbm,
    gw_hbm,
    uw_hbm,
    ow_hbm,
    mixed_hbm,
    token_grad_hbm,
    proj_hbm,
    gate_grad_hbm,
    up_grad_hbm,
    out_grad_hbm,
    tokens_ref,
    cotan_ref,
    down_ref,
    up_ref,
    gw_ref,
    uw_ref,
    ow_ref,
    mixed_ref,
    token_grad_ref,
    gate_grad_ref,
    up_grad_ref,
    out_grad_ref,
    load_sem,
    store_sem,
    mid,
    sides,
    lates,
    term_sum,
    x_out,
    x_in,
    x_sum,
    z_out,
    z_in,
    last_out,
    gathered,
    send_rows,
    expert_rows,
    result_rows,
    back_rows,
    pick,
    weigh,
    extra_sum,
    act,
    grad_gate,
    grad_up,
    ring_out,
    ring_in,
    grads_out,
    grads_in,
    grads_half,
    gather_send,
    gather_recv,
    slot_send,
    slot_recv,
    back_send,
    back_recv,
    own_sem,
    ring_send,
    ring_recv,
    grad_send,
    grad_recv,
    half_send,
    half_recv,
    side_send,
    side_recv,
    relay_send,
    late_send,
    late_recv,
    x_send,
    x_recv,
    z_send,
    z_recv,
    last_send,
    last_recv,
):
    tokens_here, latent = tokens_ref.shape[0], down_ref.shape[1]
    hidden = gw_ref.shape[1]
    experts = lax.axis_size("expert")
    groups = lax.axis_size("dp")
    columns = experts // (ring * CORES)
    peers = columns * CORES
    half = ring // 2
    sets = ring // SET
    me = lax.axis_index("expert")
    my_group = lax.axis_index("dp")
    z = lax.rem(lax.div(me, CORES), ring)
    core = lax.rem(me, CORES)
    place = lax.div(me, ring * CORES) * CORES + core

    def on_ring(step):
        other = lax.rem(z + step + ring, ring)
        return (my_group, me + (other - z) * CORES)

    def at_peer(d):
        return (my_group, (lax.div(d, CORES) * ring + z) * CORES + lax.rem(d, CORES))

    def peer(j):
        return lax.rem(place + j, peers)

    def group_at(k):
        return (lax.rem(my_group + k, groups), me)

    def mate(k, c):
        return (lax.rem(my_group + k, groups), me - core + c)

    mates = [(k, c) for k in range(1, groups) for c in range(CORES)] + [(0, 1 - core)]

    barrier = pltpu.get_barrier_semaphore()
    for step in range(1, ring):
        pl.semaphore_signal(barrier, inc=1, device_id=on_ring(step), device_id_type=MESH)
    for j in range(1, peers):
        pl.semaphore_signal(barrier, inc=1, device_id=at_peer(peer(j)), device_id_type=MESH)
    for k, c in mates:
        pl.semaphore_signal(barrier, inc=1, device_id=mate(k, c), device_id_type=MESH)

    loads = [
        pltpu.make_async_copy(src, dst, load_sem.at[n])
        for n, (src, dst) in enumerate(
            (
                (tokens_hbm, tokens_ref),
                (down_hbm, down_ref),
                (cotan_hbm, cotan_ref),
                (up_hbm, up_ref),
                (gw_hbm, gw_ref),
                (uw_hbm, uw_ref),
                (ow_hbm, ow_ref),
            )
        )
    ]
    stores = [
        pltpu.make_async_copy(src, dst, store_sem.at[n])
        for n, (src, dst) in enumerate(
            (
                (mixed_ref, mixed_hbm),
                (token_grad_ref, token_grad_hbm),
                (gate_grad_ref, gate_grad_hbm),
                (up_grad_ref, up_grad_hbm),
                (out_grad_ref, out_grad_hbm),
            )
        )
    ]
    for load in loads[:2]:
        load.start()

    expert_ids = lax.broadcasted_iota(jnp.int32, (experts, tokens_here), 0)
    table = jnp.zeros((experts, tokens_here), F32)
    for k in range(routes_ref.shape[0]):
        table = table + jnp.where(expert_ids == routes_ref[k : k + 1, :], gates_ref[k : k + 1, :], 0.0)
    table = table.astype(BF16)
    per_column = ring * CORES
    for b in range(columns):
        rows = slice(b * per_column, (b + 1) * per_column)
        lanes = slice(b * tokens_here, (b + 1) * tokens_here)
        gathered[0, tokens_here : tokens_here + per_column, lanes] = table[rows, :]

    def gather_copy(way, step, part):
        source = 0 if step == 0 else 2 * step - 1 + way
        target = 2 * step + 1 + way if step < half - 1 else ring - 1
        rows = pl.ds(0, tokens_here + MAIN if part == 0 else tokens_here)
        lanes = pl.ds(part * latent, latent)
        return pltpu.make_async_remote_copy(
            src_ref=gathered.at[source, rows, lanes],
            dst_ref=gathered.at[target, rows, lanes],
            send_sem=gather_send.at[way, step, part],
            recv_sem=gather_recv.at[way, step, part],
            device_id=on_ring(1 if way == 0 else -1),
            device_id_type=MESH,
        )

    def gather_pieces(step):
        return [(way, part) for part in range(2) for way in range(2) if step < half - 1 or part == way]

    loads[0].wait()
    loads[1].wait()
    for load in loads[2:4]:
        load.start()
    gathered[0, 0:tokens_here, 0:latent] = dot(tokens_ref[...], down_ref[...]).astype(BF16)
    pl.semaphore_wait(barrier, (ring - 1) + (peers - 1) + len(mates))
    for way in range(2):
        gather_copy(way, 0, 0).start()
    loads[2].wait()
    loads[3].wait()
    gathered[0, 0:tokens_here, latent:] = dot(cotan_ref[...], up_ref[...]).astype(BF16)
    for way in range(2):
        gather_copy(way, 0, 1).start()
    for load in loads[4:]:
        load.start()

    earlier = (
        lax.broadcasted_iota(jnp.int32, (tokens_here, tokens_here), 0)
        < lax.broadcasted_iota(jnp.int32, (tokens_here, tokens_here), 1)
    ).astype(BF16)
    row_ids = lax.broadcasted_iota(jnp.int32, (per_column, tokens_here), 0)
    main_slots = lax.broadcasted_iota(jnp.int32, (MAIN, tokens_here), 0).astype(F32)

    last_set = sets - 1
    near_rows = (SET - 1) * MAIN
    chunks = [(s * SET_ROWS, SET_ROWS) for s in range(last_set)] + [
        (last_set * SET_ROWS, near_rows),
        (last_set * SET_ROWS + near_rows, SET_ROWS - near_rows),
    ]

    def chunk_of(i):
        return i // SET + (1 if i == ring - 1 else 0)

    def slot_copy(j, chunk, first, count, lanes):
        d = peer(j)
        rows = pl.ds(first, count)
        return pltpu.make_async_remote_copy(
            src_ref=send_rows.at[d, rows, lanes],
            dst_ref=expert_rows.at[place, rows, lanes],
            send_sem=slot_send.at[chunk, j],
            recv_sem=slot_recv.at[chunk, j],
            device_id=at_peer(d),
            device_id_type=MESH,
        )

    def own_slots(chunk, first, count, lanes):
        rows = pl.ds(first, count)
        return pltpu.make_async_copy(
            send_rows.at[place, rows, lanes], expert_rows.at[place, rows, lanes], own_sem.at[0, chunk]
        )

    all_lanes = pl.ds(0, 2 * latent)

    def table_rows(i):
        found = []
        for b in range(columns):
            first = b * tokens_here
            info = gathered[i, tokens_here : tokens_here + per_column, first : first + tokens_here].astype(F32)
            for c in range(CORES):
                found.append(jnp.sum(jnp.where(row_ids == z * CORES + c, info, 0.0), axis=0, keepdims=True))
        return jnp.concatenate(found, axis=0)

    main_count = peers * MAIN

    def dispatch(i, part):
        s, within = i // SET, i % SET
        lanes = slice(part * latent, (part + 1) * latent)
        if part == 0:
            named = table_rows(i) > 0.0
            before = dot(named.astype(F32).astype(BF16), earlier)
            slot = jnp.where(named, before, -1.0)
            extra_rows = lax.broadcasted_iota(jnp.int32, (MAIN, tokens_here), 0)
            extra_slots = jnp.where(
                lax.div(extra_rows, EXTRA) == within, MAIN + lax.rem(extra_rows, EXTRA), -2
            ).astype(F32)
            hits = []
            for slots in (main_slots, extra_slots):
                for d in range(peers):
                    hits.append((slots == slot[d : d + 1, :]).astype(F32))
            chosen = jnp.concatenate(hits, axis=0).astype(BF16)
            pick[i] = chosen
            rows = dot(chosen, gathered[i, 0:tokens_here, lanes])
        else:
            weight = table_rows(i)
            weight_rows = jnp.concatenate(
                [jnp.broadcast_to(weight[d : d + 1, :], (MAIN, tokens_here)) for d in range(peers)], axis=0
            )
            chosen = pick[i]
            weighted = chosen.astype(F32) * jnp.concatenate([weight_rows, weight_rows], axis=0)
            weigh[i] = weighted.astype(BF16)
            scale = jnp.sum(weighted, axis=1, keepdims=True)
            rows = dot(chosen, gathered[i, 0:tokens_here, lanes]) * scale
        first = s * SET_ROWS + within * MAIN
        send_rows[:, first : first + MAIN, lanes] = rows[:main_count].astype(BF16).reshape(peers, MAIN, latent)
        extra = rows[main_count:]
        if within > 0:
            extra = extra + extra_sum[:, lanes]
        if within < SET - 1:
            extra_sum[:, lanes] = extra
        else:
            first = s * SET_ROWS + SET * MAIN
            send_rows[:, first : first + MAIN, lanes] = extra.astype(BF16).reshape(peers, MAIN, latent)
        count = MAIN if within < SET - 1 else 2 * MAIN
        lanes = pl.ds(part * latent, latent)

        def start(j, carry):
            slot_copy(j, chunk_of(i), s * SET_ROWS + within * MAIN, count, lanes).start()
            return carry

        lax.fori_loop(1, peers, start, 0)
        own_slots(chunk_of(i), s * SET_ROWS + within * MAIN, count, lanes).start()

    def side_copy(k, c, source):
        return pltpu.make_async_remote_copy(
            src_ref=source,
            dst_ref=sides.at[k, core],
            send_sem=side_send.at[k, c],
            recv_sem=side_recv.at[k, core],
            device_id=mate(k, c),
            device_id_type=MESH,
        )

    def side_arrived(k, c):
        pltpu.make_async_remote_copy(
            src_ref=tokens_ref,
            dst_ref=sides.at[k, c],
            send_sem=side_send.at[k, c],
            recv_sem=side_recv.at[k, c],
            device_id=mate(k, c),
            device_id_type=MESH,
        ).wait_recv()

    across = groups // 2

    def relay_copy(c):
        step = 1 - 2 * core
        return pltpu.make_async_remote_copy(
            src_ref=sides.at[1 + (groups - 2) * core, c],
            dst_ref=sides.at[across, c],
            send_sem=relay_send.at[c],
            recv_sem=side_recv.at[across, c],
            device_id=(lax.rem(my_group + step + groups, groups), me),
            device_id_type=MESH,
        )

    for part in range(2):
        dispatch(0, part)
    near = sorted({1, groups - 1})
    for k in near:
        for c, source in enumerate((tokens_ref, cotan_ref)):
            side_copy(k, c, source).start()

    @pl.when(core == 0)
    def _():
        side_copy(0, 1, cotan_ref).start()

    @pl.when(core == 1)
    def _():
        side_copy(0, 0, tokens_ref).start()

    sides[0, core] = jnp.where(core == 0, tokens_ref[...], cotan_ref[...])
    for step in range(1, half):
        for part in range(2):
            for way in range(2):
                gather_copy(way, step - 1, part).wait_recv()
                if (way, part) in gather_pieces(step):
                    gather_copy(way, step, part).start()
            for way in range(2):
                dispatch(2 * step - 1 + way, part)

    back_pieces = [((SET - 1) * MAIN, 2 * MAIN)] + [(n * MAIN, MAIN) for n in range(SET - 2, -1, -1)]

    def back_copy(j, s, n):
        d = peer(j)
        first, count = back_pieces[n]
        rows = pl.ds(s * SET_ROWS + first, count)
        return pltpu.make_async_remote_copy(
            src_ref=result_rows.at[d, rows],
            dst_ref=back_rows.at[place, rows],
            send_sem=back_send.at[s, n, j],
            recv_sem=back_recv.at[s, n, j],
            device_id=at_peer(d),
            device_id_type=MESH,
        )

    def own_back(s, n):
        first, count = back_pieces[n]
        rows = pl.ds(s * SET_ROWS + first, count)
        return pltpu.make_async_copy(result_rows.at[place, rows], back_rows.at[place, rows], own_sem.at[1 + n, s])

    tile = min(256, hidden)
    wide = min(256, latent)
    def send_back(s, n):
        def start(j, carry):
            back_copy(j, s, n).start()
            return carry

        lax.fori_loop(1, peers, start, 0)
        own_back(s, n).start()

    def slots_arrived(chunk):
        def arrived(j, carry):
            slot_copy(j, chunk, *chunks[chunk], all_lanes).wait_recv()
            return carry

        lax.fori_loop(1, peers, arrived, 0)
        own_slots(chunk, *chunks[chunk], all_lanes).wait()

    def expert(chunk):
        first, per_peer = chunks[chunk]
        set_rows = slice(first, first + per_peer)
        count = peers * per_peer

        def hidden_tile(h, carry):
            cols = pl.ds(pl.multiple_of(h * tile, tile), tile)
            rows_in = expert_rows[:, set_rows, 0:latent].reshape(count, latent)
            grad_in = expert_rows[:, set_rows, latent:].reshape(count, latent)
            pre_gate = dot(rows_in, gw_ref[:, cols])
            pre_up = dot(rows_in, uw_ref[:, cols])
            grad_act = dot(grad_in, ow_ref[cols, :], COLS)
            sig = 1.0 / (1.0 + jnp.exp(-pre_gate))
            swish = pre_gate * sig
            shape = (peers, per_peer, tile)
            act[:, set_rows, cols] = (swish * pre_up).astype(BF16).reshape(shape)
            grad_gate[:, set_rows, cols] = (
                (grad_act * pre_up * (sig * (1.0 + pre_gate * (1.0 - sig)))).astype(BF16).reshape(shape)
            )
            grad_up[:, set_rows, cols] = (grad_act * swish).astype(BF16).reshape(shape)
            return carry

        lax.fori_loop(0, hidden // tile, hidden_tile, 0)

        def latent_tile(n, carry):
            cols = pl.ds(pl.multiple_of(n * wide, wide), wide)
            later = pl.ds(pl.multiple_of(latent + n * wide, wide), wide)
            shape = (peers, per_peer, wide)
            out = dot(act[:, set_rows, :].reshape(count, hidden), ow_ref[:, cols])
            result_rows[:, set_rows, cols] = out.astype(BF16).reshape(shape)
            back = dot(grad_gate[:, set_rows, :].reshape(count, hidden), gw_ref[cols, :], COLS)
            back = back + dot(grad_up[:, set_rows, :].reshape(count, hidden), uw_ref[cols, :], COLS)
            result_rows[:, set_rows, later] = back.astype(BF16).reshape(shape)
            return carry

        lax.fori_loop(0, latent // wide, latent_tile, 0)


    for load in loads[4:]:
        load.wait()
    for chunk in range(last_set):
        slots_arrived(chunk)
        expert(chunk)
    for way, part in gather_pieces(half - 1):
        gather_copy(way, half - 1, part).wait_recv()
    for part in range(2):
        dispatch(ring - 1, part)
    slots_arrived(last_set)
    expert(last_set)
    slots_arrived(last_set + 1)
    for s in range(last_set):
        send_back(s, 0)
    expert(last_set + 1)
    send_back(last_set, 0)
    send_back(last_set, 1)
    send_back(last_set, 2)
    send_back(last_set, 3)
    for s in range(last_set):
        for n in range(1, SET):
            send_back(s, n)

    for c in range(CORES):
        for k in near:
            side_arrived(k, c)
    if across > 1:
        for c in range(CORES):
            relay_copy(c).start()

    share = hidden // groups
    all_rows = peers * sets * SET_ROWS

    def grad_copy(k):
        return pltpu.make_async_remote_copy(
            src_ref=grads_out.at[k],
            dst_ref=grads_in.at[k],
            send_sem=grad_send.at[k],
            recv_sem=grad_recv.at[k],
            device_id=group_at(k),
            device_id_type=MESH,
        )

    def weight_terms(k):
        cols = pl.ds(pl.multiple_of(lax.rem(my_group + k, groups) * share, share), share)
        rows_in = expert_rows[:, :, 0:latent].reshape(all_rows, latent)
        grad_in = expert_rows[:, :, latent:].reshape(all_rows, latent)
        gate_term = dot(rows_in, grad_gate[:, :, cols].reshape(all_rows, share), ROWS)
        up_term = dot(rows_in, grad_up[:, :, cols].reshape(all_rows, share), ROWS)
        out_term = dot(act[:, :, cols].reshape(all_rows, share), grad_in, ROWS)
        return gate_term, up_term, out_term

    def other_share(k, carry):
        gate_term, up_term, out_term = weight_terms(k)
        grads_out[k, 0:latent, 0:share] = gate_term.astype(BF16)
        grads_out[k, 0:latent, share:] = up_term.astype(BF16)
        grads_out[k, latent:, :] = out_term.astype(BF16)
        return carry

    half_rows = (latent + share) // 2

    def pass_copy(way):
        return pltpu.make_async_remote_copy(
            src_ref=grads_out.at[across, pl.ds(way * half_rows, half_rows)],
            dst_ref=grads_half.at[way],
            send_sem=half_send.at[way],
            recv_sem=half_recv.at[way],
            device_id=group_at(near[way]),
            device_id_type=MESH,
        )

    if across > 1:
        lax.fori_loop(across, across + 1, other_share, 0)
        for way in range(2):
            pass_copy(way).start()
    lax.fori_loop(0, len(near), lambda n, carry: other_share(1 + (groups - 2) * n, carry), 0)

    def combine(i):
        s, within = i // SET, i % SET
        first = s * SET_ROWS + within * MAIN
        extra = s * SET_ROWS + SET * MAIN
        shape = (peers * MAIN, latent)
        parts = []
        for part, matrix in enumerate((weigh, pick)):
            lanes = slice(part * latent, (part + 1) * latent)
            rows = jnp.concatenate(
                [
                    back_rows[:, first : first + MAIN, lanes].reshape(shape),
                    back_rows[:, extra : extra + MAIN, lanes].reshape(shape),
                ],
                axis=0,
            )
            parts.append(dot(matrix[i], rows, ROWS))
        return parts

    def ring_copy(way, step, part):
        lanes = pl.ds(part * latent, latent)
        return pltpu.make_async_remote_copy(
            src_ref=ring_out.at[way, step, :, lanes],
            dst_ref=ring_in.at[way, step, :, lanes],
            send_sem=ring_send.at[way, step, part],
            recv_sem=ring_recv.at[way, step, part],
            device_id=on_ring(-1 if way == 0 else 1),
            device_id_type=MESH,
        )

    def ring_pieces(step):
        pieces = [(way, 1 - way) for way in range(2)] if step > 0 else []
        return pieces + [(way, way) for way in range(2)]

    arrived_pieces = set()

    def ready(i):
        s = i // SET
        n = SET - 1 - i % SET
        if (s, n) in arrived_pieces:
            return
        arrived_pieces.add((s, n))

        def arrived(j, carry):
            back_copy(j, s, n).wait_recv()
            return carry

        lax.fori_loop(1, peers, arrived, 0)
        own_back(s, n).wait()

    ready(ring - 1)
    parts = combine(ring - 1)
    for way, part in ring_pieces(0):
        ring_out[way, 0, :, part * latent : (part + 1) * latent] = parts[part].astype(BF16)
        ring_copy(way, 0, part).start()
    gate_grad_ref[...], up_grad_ref[...], out_grad_ref[...] = weight_terms(0)
    for way, k in enumerate(near):
        if across > 1:
            pass_copy(way).wait_recv()
            rows = slice(way * half_rows, (way + 1) * half_rows)
            grads_out[k, rows, :] = (grads_out[k, rows, :].astype(F32) + grads_half[way].astype(F32)).astype(BF16)
        grad_copy(k).start()
    for step in range(1, half):
        parts = []
        for way in range(2):
            i = 2 * (half - step) - 1 + way
            ready(i)
            parts.append(combine(i))
        for way, part in ring_pieces(step):
            lanes = slice(part * latent, (part + 1) * latent)
            value = parts[way][part]
            if (way, part) in ring_pieces(step - 1):
                ring_copy(way, step - 1, part).wait_recv()
                value = value + ring_in[way, step - 1, :, lanes].astype(F32)
            ring_out[way, step, :, lanes] = value.astype(BF16)
            ring_copy(way, step, part).start()
    block = latent // groups
    features = tokens_ref.shape[1]
    column_rows = features // columns
    ring_rows = column_rows // ring
    last_rows = ring_rows // CORES

    def late_lanes(k, c):
        start = latent * (1 - c) + block * lax.rem(my_group + k, groups)
        return pl.ds(pl.multiple_of(start, block), block)

    def late_copy(k, c):
        return pltpu.make_async_remote_copy(
            src_ref=mid.at[:, late_lanes(k, c)],
            dst_ref=lates.at[k, core],
            send_sem=late_send.at[k, c],
            recv_sem=late_recv.at[k, core],
            device_id=mate(k, c),
            device_id_type=MESH,
        )

    def late_arrived(k, c):
        pltpu.make_async_remote_copy(
            src_ref=lates.at[k, c],
            dst_ref=lates.at[k, c],
            send_sem=late_send.at[k, c],
            recv_sem=late_recv.at[k, c],
            device_id=mate(k, c),
            device_id_type=MESH,
        ).wait_recv()

    ready(0)
    parts = combine(0)
    for part in range(2):
        lanes = slice(part * latent, (part + 1) * latent)
        value = parts[part]
        for way in range(2):
            if (way, part) in ring_pieces(half - 1):
                ring_copy(way, half - 1, part).wait_recv()
                value = value + ring_in[way, half - 1, :, lanes].astype(F32)
        mid[:, lanes] = value.astype(BF16)
        for k in range(1, groups):
            late_copy(k, 1 - part).start()
    late_copy(0, 1 - core).start()
    lates[0, core] = mid[:, late_lanes(0, core)]

    pair = CORES * tokens_here

    def late_columns(k):
        return lates[k].reshape(pair, block).astype(F32).T.astype(BF16)

    side_arrived(0, 1 - core)
    late_arrived(0, 1 - core)
    term_sum[...] = dot(late_columns(0), sides[0].reshape(pair, features))
    for k in near:
        if k != across:
            for c in range(CORES):
                late_arrived(k, c)
            term_sum[...] += dot(late_columns(k), sides[k].reshape(pair, features))
    for c in range(CORES):
        if across > 1:
            side_arrived(across, c)
        late_arrived(across, c)
    last_columns = late_columns(across)

    def term_rows(k):
        first = lax.rem(lax.div(me, ring * CORES) + k, columns) * column_rows
        cols = pl.ds(pl.multiple_of(first, column_rows), column_rows)
        term = dot(last_columns, sides[across, :, :, cols].reshape(pair, column_rows))
        return (term_sum[:, cols] + term).T

    def x_copy(k):
        return pltpu.make_async_remote_copy(
            src_ref=x_out.at[k],
            dst_ref=x_in.at[k],
            send_sem=x_send.at[k],
            recv_sem=x_recv.at[k],
            device_id=at_peer(peer(k * CORES)),
            device_id_type=MESH,
        )

    for k in sorted(range(1, columns), key=lambda k: -min(k, columns - k)):
        x_out[k] = term_rows(k).astype(BF16)
        x_copy(k).start()
    total = term_rows(0)
    mixed_ref[...] = dot(mid[:, 0:latent], up_ref[...], COLS)
    stores[0].start()
    token_grad_ref[...] = dot(mid[:, latent:], down_ref[...], COLS)
    stores[1].start()
    for k in near:
        grad_copy(k).wait_recv()
        gate_grad_ref[...] += grads_in[k, 0:latent, 0:share].astype(F32)
        up_grad_ref[...] += grads_in[k, 0:latent, share:].astype(F32)
        out_grad_ref[...] += grads_in[k, latent:, :].astype(F32)
    for store in stores[2:]:
        store.start()
    for k in range(1, columns):
        x_copy(k).wait_recv()
        total = total + x_in[k].astype(F32)
    x_sum[...] = total.reshape(ring, ring_rows, block)
    z_out[...] = x_sum[...].astype(BF16)

    def z_copy(r):
        return pltpu.make_async_remote_copy(
            src_ref=z_out.at[lax.rem(z + r, ring)],
            dst_ref=z_in.at[r],
            send_sem=z_send.at[r],
            recv_sem=z_recv.at[r],
            device_id=on_ring(r),
            device_id_type=MESH,
        )

    for r in range(1, ring):
        z_copy(r).start()
    total = x_sum[z]
    for r in range(1, ring):
        z_copy(r).wait_recv()
        total = total + z_in[r].astype(F32)
    last_out[...] = total.reshape(CORES, last_rows, block)

    def group_lanes(k):
        return pl.ds(pl.multiple_of(lax.rem(my_group + groups - k, groups) * block, block), block)

    def last_copy(k, c):
        return pltpu.make_async_remote_copy(
            src_ref=last_out.at[c],
            dst_ref=proj_hbm.at[core, :, group_lanes(0)],
            send_sem=last_send.at[k, c],
            recv_sem=last_recv.at[k, core],
            device_id=mate(k, c),
            device_id_type=MESH,
        )

    def last_arrived(k, c):
        pltpu.make_async_remote_copy(
            src_ref=last_out.at[c],
            dst_ref=proj_hbm.at[c, :, group_lanes(k)],
            send_sem=last_send.at[k, c],
            recv_sem=last_recv.at[k, c],
            device_id=mate(k, c),
            device_id_type=MESH,
        ).wait_recv()

    own_last = pltpu.make_async_copy(
        last_out.at[core], proj_hbm.at[core, :, group_lanes(0)], last_recv.at[0, core]
    )

    for k, c in mates:
        last_copy(k, c).start()
    own_last.start()

    own_last.wait()
    for k, c in mates:
        last_arrived(k, c)

    for k in near:
        for c in range(CORES):
            side_copy(k, c, tokens_ref).wait_send()
    side_copy(0, 1 - core, tokens_ref).wait_send()
    if across > 1:
        for c in range(CORES):
            relay_copy(c).wait_send()
    for k, c in mates:
        late_copy(k, c).wait_send()
        last_copy(k, c).wait_send()
    for k in range(1, columns):
        x_copy(k).wait_send()
    for r in range(1, ring):
        z_copy(r).wait_send()

    for step in range(half):
        for way, part in gather_pieces(step):
            gather_copy(way, step, part).wait_send()
        for way, part in ring_pieces(step):
            ring_copy(way, step, part).wait_send()

    def sent(j, carry):
        for chunk in range(len(chunks)):
            slot_copy(j, chunk, *chunks[chunk], all_lanes).wait_send()
        for s in range(sets):
            for n in range(SET):
                back_copy(j, s, n).wait_send()
        return carry

    lax.fori_loop(1, peers, sent, 0)
    for k in near:
        grad_copy(k).wait_send()
    if across > 1:
        for way in range(2):
            pass_copy(way).wait_send()
    for store in stores:
        store.wait()


def layer(ring, routes, gates, tokens, cotan, down, up, gate_weight, up_weight, out_weight):
    count, latent = tokens.shape[0], down.shape[1]
    hidden = gate_weight.shape[1]
    experts = lax.axis_size("expert")
    groups = lax.axis_size("dp")
    peers = experts // ring
    sets = ring // SET
    half = ring // 2
    share = hidden // groups
    chosen = 2 * peers * MAIN
    rows = sets * SET_ROWS
    features = tokens.shape[1]
    columns = peers // CORES
    block = latent // groups
    last_rows = features // experts
    ring_rows = last_rows * CORES
    vmem = pl.BlockSpec(memory_space=pltpu.VMEM)
    anywhere = pl.BlockSpec(memory_space=pl.ANY)
    dma = pltpu.SemaphoreType.DMA
    arrays = (tokens, cotan, down, up, gate_weight, up_weight, out_weight)
    results = (
        jax.ShapeDtypeStruct((count, features), F32),
        jax.ShapeDtypeStruct((count, features), F32),
        jax.ShapeDtypeStruct((CORES, last_rows, latent), F32),
        jax.ShapeDtypeStruct((latent, share), F32),
        jax.ShapeDtypeStruct((latent, share), F32),
        jax.ShapeDtypeStruct((share, latent), F32),
    )
    return pl.pallas_call(
        partial(layer_kernel, ring),
        out_shape=results,
        in_specs=[vmem] * 2 + [anywhere] * 7,
        out_specs=(anywhere,) * len(results),
        scratch_shapes=[pltpu.VMEM(a.shape, a.dtype) for a in arrays + results[:2] + results[3:]]
        + [
            dma((len(arrays),)),
            dma((len(results) - 1,)),
            pltpu.VMEM((count, 2 * latent), BF16),
            pltpu.VMEM((groups, CORES, count, features), BF16),
            pltpu.VMEM((groups, CORES, count, block), BF16),
            pltpu.VMEM((block, features), F32),
            pltpu.VMEM((columns, features // columns, block), BF16),
            pltpu.VMEM((columns, features // columns, block), BF16),
            pltpu.VMEM((ring, ring_rows, block), F32),
            pltpu.VMEM((ring, ring_rows, block), BF16),
            pltpu.VMEM((ring, ring_rows, block), BF16),
            pltpu.VMEM((CORES, last_rows, block), F32),
            pltpu.VMEM((ring, count + MAIN, 2 * latent), BF16),
            pltpu.VMEM((peers, rows, 2 * latent), BF16),
            pltpu.VMEM((peers, rows, 2 * latent), BF16),
            pltpu.VMEM((peers, rows, 2 * latent), BF16),
            pltpu.VMEM((peers, rows, 2 * latent), BF16),
            pltpu.VMEM((ring, chosen, count), BF16),
            pltpu.VMEM((ring, chosen, count), BF16),
            pltpu.VMEM((peers * MAIN, 2 * latent), F32),
            pltpu.VMEM((peers, rows, hidden), BF16),
            pltpu.VMEM((peers, rows, hidden), BF16),
            pltpu.VMEM((peers, rows, hidden), BF16),
            pltpu.VMEM((2, half, count, 2 * latent), BF16),
            pltpu.VMEM((2, half, count, 2 * latent), BF16),
            pltpu.VMEM((groups, latent + share, 2 * share), BF16),
            pltpu.VMEM((groups, latent + share, 2 * share), BF16),
            pltpu.VMEM((2, (latent + share) // 2, 2 * share), BF16),
            dma((2, half, 2)),
            dma((2, half, 2)),
            dma((sets + 1, peers)),
            dma((sets + 1, peers)),
            dma((sets, SET, peers)),
            dma((sets, SET, peers)),
            dma((1 + SET, sets + 1)),
            dma((2, half, 2)),
            dma((2, half, 2)),
            dma((groups,)),
            dma((groups,)),
            dma((2,)),
            dma((2,)),
            dma((groups, CORES)),
            dma((groups, CORES)),
            dma((CORES,)),
            dma((groups, CORES)),
            dma((groups, CORES)),
            dma((columns,)),
            dma((columns,)),
            dma((ring,)),
            dma((ring,)),
            dma((groups, CORES)),
            dma((groups, CORES)),
        ],
        compiler_params=pltpu.CompilerParams(
            collective_id=0, has_side_effects=True, vmem_limit_bytes=60 * 1024 * 1024
        ),
        name="layer",
    )(routes, gates, tokens, cotan, down, up, gate_weight, up_weight, out_weight)


def shards(
    ring,
    tokens,
    routes,
    gate_values,
    latent_down,
    gate_weight,
    up_weight,
    out_weight,
    latent_up,
    grad_mixed,
):
    mixed, grad_tokens, proj_grads, gate_grad, up_grad, out_grad = layer(
        ring,
        routes.T,
        gate_values.T,
        tokens,
        grad_mixed,
        latent_down,
        latent_up,
        gate_weight[0],
        up_weight[0],
        out_weight[0],
    )
    mixed, grad_tokens = mixed.astype(BF16), grad_tokens.astype(BF16)
    return mixed, grad_tokens, proj_grads[0], proj_grads[1], gate_grad[None], up_grad[None], out_grad[None]


def solution(mesh, ring=RING):
    rows = P(("dp", "expert"), None)
    own = P("expert", None, None)
    return jax.shard_map(
        partial(shards, ring),
        mesh=mesh,
        in_specs=(rows, rows, rows, P(), own, own, own, P(), rows),
        out_specs=(
            rows,
            rows,
            P("expert", None),
            P("expert", None),
            P("expert", None, "dp"),
            P("expert", None, "dp"),
            P("expert", "dp", None),
        ),
        check_vma=False,
    )
```
